32 devices in a mesh: dp: 16 (over z, y, core), blk: 2 (over x).
Axes of the slice: x: 2, y: 2, z: 4, core: 2. Of those that a mesh axis runs over, the one named last changes fastest.
Arguments:
- hidden_in: bfloat16 [8192, 768], P(('dp', 'blk')), may hold values from -6 to 6
- cotangent: bfloat16 [8192, 768], P(('dp', 'blk')), may hold values from -6 to 6
- lengths: int32 [16], P('dp'), may hold values from 320 to 480, as said below
- coords: int32 [2, 8192], P(None, ('dp', 'blk')), may hold values from 0 to 1000
- qkv_weight: bfloat16 [2, 768, 2304], P(None, ('dp', 'blk')), may hold values from -0.21875 to 0.21875
- query_bias: bfloat16 [2, 768], P(None, ('dp', 'blk')), may hold values from -3 to 3
- value_bias: bfloat16 [2, 768], P(None, ('dp', 'blk')), may hold values from -3 to 3
- out_weight: bfloat16 [2, 768, 768], P(None, ('dp', 'blk')), may hold values from -1.25 to 1.25
- out_bias: bfloat16 [2, 768], P(None, ('dp', 'blk')), may hold values from -3 to 3
- norm1_gain: bfloat16 [2, 768], P(None, ('dp', 'blk')), may hold values from 0.099609375 to 1.8984375
- norm1_shift: bfloat16 [2, 768], P(None, ('dp', 'blk')), may hold values from -2 to 2
- in_weight: bfloat16 [2, 768, 3072], P(None, ('dp', 'blk')), may hold values from -0.21875 to 0.21875
- in_bias: bfloat16 [2, 3072], P(None, ('dp', 'blk')), may hold values from -3 to 3
- back_weight: bfloat16 [2, 3072, 768], P(None, ('dp', 'blk')), may hold values from -0.109375 to 0.109375
- back_bias: bfloat16 [2, 768], P(None, ('dp', 'blk')), may hold values from -3 to 3
- norm2_gain: bfloat16 [2, 768], P(None, ('dp', 'blk')), may hold values from 0.099609375 to 1.8984375
- norm2_shift: bfloat16 [2, 768], P(None, ('dp', 'blk')), may hold values from -2 to 2
- line_table: bfloat16 [32, 12], replicated, may hold values from -3 to 3
- horizontal_table: bfloat16 [64, 12], replicated, may hold values from -3 to 3
- vertical_table: bfloat16 [64, 12], replicated, may hold values from -3 to 3
Outputs:
- hidden_out: bfloat16 [8192, 768], P(('dp', 'blk'))
- grad_in: bfloat16 [8192, 768], P(('dp', 'blk'))
- grad_qkv_weight: float32 [2, 768, 2304], P(None, ('dp', 'blk'))
- grad_query_bias: float32 [2, 768], P(None, ('dp', 'blk'))
- grad_value_bias: float32 [2, 768], P(None, ('dp', 'blk'))
- grad_out_weight: float32 [2, 768, 768], P(None, ('dp', 'blk'))
- grad_out_bias: float32 [2, 768], P(None, ('dp', 'blk'))
- grad_norm1_gain: float32 [2, 768], P(None, ('dp', 'blk'))
- grad_norm1_shift: float32 [2, 768], P(None, ('dp', 'blk'))
- grad_in_weight: float32 [2, 768, 3072], P(None, ('dp', 'blk'))
- grad_in_bias: float32 [2, 3072], P(None, ('dp', 'blk'))
- grad_back_weight: float32 [2, 3072, 768], P(None, ('dp', 'blk'))
- grad_back_bias: float32 [2, 768], P(None, ('dp', 'blk'))
- grad_norm2_gain: float32 [2, 768], P(None, ('dp', 'blk'))
- grad_norm2_shift: float32 [2, 768], P(None, ('dp', 'blk'))
- grad_line_table: float32 [32, 12], replicated
- grad_horizontal_table: float32 [64, 12], replicated
- grad_vertical_table: float32 [64, 12], replicated
The draws below stay inside these ranges and needn't reach their ends.
Inputs may be any that keep to these rules, and one draw needn't show every extreme that they name: `lengths`: each entry is the number of real tokens of the one document of a group; they are the first of the group's 512 slots and the rest are padding.
All inputs are finite; a program needn't handle non-finite values.
Results may differ from the reference program's by a relative error of at most 0.029.
Values may be sent and summed in bfloat16 or wider, within the bound.
No kernel may reach another device: no remote copies, remote signals or barrier semaphores. Data moves between devices by JAX's collectives and lax.ppermute only.
A program may use at most 256 MiB of HBM per device.

```python
import math
import jax
import jax.numpy as jnp
from jax import lax

D = 768
HEADS = 12
FF = 3072
LAYERS = 2
BUCKETS_1D = 32
BUCKETS_2D = 64
REACH_1D = 128
REACH_2D = 256
TOK_DEV = 256
GROUPS = 16
SEQ = 512
TOKENS = 8192


def draw_lengths(key, part):
    key_value, key_pick, key_other = jax.random.split(key, 3)
    low_length = TOK_DEV + TOK_DEV // 4
    high_length = SEQ - TOK_DEV // 8
    drawn = jax.random.randint(key_value, (GROUPS,), low_length, high_length + 1)
    chosen = jax.random.randint(key_pick, (), 0, GROUPS)
    second = (chosen + jax.random.randint(key_other, (), 1, GROUPS)) % GROUPS
    places = jnp.arange(GROUPS)
    drawn = jnp.where(places == chosen, high_length, drawn)
    drawn = jnp.where(places == second, low_length, drawn)
    return drawn.astype(jnp.int32)


def touch_ends(entries, own_key, least, high):
    shape = entries.shape
    spot = [jax.random.randint(jax.random.fold_in(own_key, axis), (), 0, shape[axis]) for axis in range(len(shape))]
    entries = entries.at[tuple(spot)].set(least)
    longest = shape.index(max(shape))
    spot[longest] = (spot[longest] + 1) % shape[longest]
    return entries.at[tuple(spot)].set(high)


def raised(entries, rng, source, target, blocks, factor):
    def block_of(position):
        return (jnp.arange(entries.shape[position]) // (entries.shape[position] // blocks)).reshape((-1,) + (1,) * (entries.ndim - 1 - position))

    first = jax.random.permutation(rng, blocks)[block_of(target)]
    other_side = (block_of(target) + blocks // 2) % blocks
    return jnp.where((block_of(source) == first) | (block_of(source) == other_side), factor * entries, entries)


def block_levels(rng, extent, shards, low, top_value):
    def one(dim, shards_of):
        steps = jax.random.uniform(jax.random.fold_in(jax.random.fold_in(rng, 6), dim), (shards_of,), jnp.float32, low / len(shards), top_value / len(shards))
        return jnp.repeat(jnp.exp(steps), extent[dim] // shards_of).reshape((-1,) + (1,) * (len(extent) - dim - 1))

    level = one(*shards[0])
    for cut in shards[1:]:
        level = level * one(*cut)
    return level


def centred(rng, dims, deviation, most, cuts=(), kind=jnp.bfloat16):
    loudness = block_levels(rng, dims, cuts, -0.22, 0.18) if cuts else 1.0
    values = jax.random.normal(rng, dims, jnp.float32) * deviation * loudness
    return jnp.minimum(jnp.maximum(values, -most), most).astype(kind)


def heavy_noise(stream_key, shape, spread, reach, pieces, heavy, held_as=jnp.bfloat16):
    values = spread * jax.random.normal(stream_key, shape, jnp.float32)
    if pieces:
        values = values * block_levels(stream_key, shape, pieces, -0.22, 0.18)
    return jnp.clip(raised(values, jax.random.fold_in(stream_key, 3), *heavy), -reach, reach).astype(held_as)


def setup_inputs(seed: int = 0) -> dict:
    key_of = jax.random.split(jax.random.key(seed), 21)
    return {
        "hidden_in": centred(key_of[0], (TOKENS, D), 1.0, 6.0, ((0, 32),)),
        "cotangent": heavy_noise(key_of[1], (TOKENS, D), 1.0, 6.0, ((0, 32),), (0, 1, 32, 2.75)),
        "lengths": draw_lengths(jax.random.fold_in(key_of[20], 71), 0),
        "coords": touch_ends(jax.random.randint(key_of[3], (2, TOKENS), 0, 1001), jax.random.fold_in(key_of[3], 1), 0, 1000).astype(jnp.int32),
        "qkv_weight": centred(key_of[4], (LAYERS, D, 3 * D), D ** -0.5, 0.21875, ((1, 32),)),
        "query_bias": centred(key_of[5], (LAYERS, D), 0.5, 3.0, ((1, 32),)),
        "value_bias": centred(key_of[6], (LAYERS, D), 0.5, 3.0, ((1, 32),)),
        "out_weight": centred(key_of[7], (LAYERS, D, D), (D // 32) ** -0.5, 1.25, ((1, 32),)),
        "out_bias": centred(key_of[8], (LAYERS, D), 0.5, 3.0, ((1, 32),)),
        "norm1_gain": jnp.clip(1.0 + 0.18 * jax.random.normal(key_of[9], (LAYERS, D), jnp.float32), 0.099609375, 1.8984375).astype(jnp.bfloat16),
        "norm1_shift": centred(key_of[10], (LAYERS, D), 0.3, 2.0, ((1, 32),)),
        "in_weight": centred(key_of[11], (LAYERS, D, FF), D ** -0.5, 0.21875, ((1, 32),)),
        "in_bias": centred(key_of[12], (LAYERS, FF), 0.5, 3.0, ((1, 32),)),
        "back_weight": centred(key_of[13], (LAYERS, FF, D), FF ** -0.5, 0.109375, ((1, 32),)),
        "back_bias": centred(key_of[14], (LAYERS, D), 0.5, 3.0, ((1, 32),)),
        "norm2_gain": jnp.clip(1.0 + 0.18 * jax.random.normal(key_of[15], (LAYERS, D), jnp.float32), 0.099609375, 1.8984375).astype(jnp.bfloat16),
        "norm2_shift": centred(key_of[16], (LAYERS, D), 0.3, 2.0, ((1, 32),)),
        "line_table": centred(key_of[17], (BUCKETS_1D, HEADS), 0.5, 3.0),
        "horizontal_table": centred(key_of[18], (BUCKETS_2D, HEADS), 0.5, 3.0),
        "vertical_table": centred(key_of[19], (BUCKETS_2D, HEADS), 0.5, 3.0),
    }


eps_norm = 1e-12
big_negative = -1e+30
highest = lax.Precision.HIGHEST

@jax.custom_vjp
def low(v):
    return lax.optimization_barrier(v.astype(jnp.bfloat16)).astype(jnp.float32)

@jax.custom_vjp
def low_back(v):
    return v

def low_keep(v):
    return (low(v), None)

def low_pass(kept, grad):
    return (grad,)

def back_keep(v):
    return (v, None)

def back_low(kept, grad):
    return (low(grad),)
low.defvjp(low_keep, low_pass)
low_back.defvjp(back_keep, back_low)

def bucket_marks(bucket_count, far_reach):
    half_count = bucket_count // 2
    exact_limit = half_count // 2
    thresholds = []
    for bucket_step in range(1, half_count):
        if bucket_step < exact_limit:
            thresholds.append(bucket_step)
        else:
            thresholds.append(math.ceil(exact_limit * (far_reach / exact_limit) ** ((bucket_step - exact_limit) / (half_count - exact_limit))))
    return thresholds

def bucket_of(offset, bucket_count, far_reach):
    magnitude = jnp.abs(offset)
    result = jnp.where(offset > 0, bucket_count // 2, 0).astype(jnp.int32)
    for threshold in bucket_marks(bucket_count, far_reach):
        result = result + (magnitude >= threshold).astype(jnp.int32)
    return result

def layer_norm(values, gain, shift):
    centered = values - lax.optimization_barrier(jnp.mean(values, axis=-1, keepdims=True))
    variance = lax.optimization_barrier(jnp.mean(centered * centered, axis=-1, keepdims=True))
    return centered * lax.rsqrt(variance + eps_norm) * gain + shift

def product(left, right):
    return jnp.dot(left, right, preferred_element_type=jnp.float32, precision=highest)

def encoder_layer(hidden, weights, score_bias, same_doc):
    qkv_weight, query_bias, value_bias, out_weight, out_bias, gain_one, shift_one, in_weight, in_bias, back_weight, back_bias, gain_two, shift_two = weights
    seq_rows, model_width = hidden.shape
    head_count = score_bias.shape[0]
    head_dim = model_width // head_count
    inputs = low(hidden)
    joined = product(inputs, qkv_weight)
    queries = low(low_back((joined[:, :model_width] + query_bias) * 0.125)).reshape(seq_rows, head_count, head_dim)
    keys = low(low_back(joined[:, model_width:2 * model_width])).reshape(seq_rows, head_count, head_dim)
    values = low(low_back(joined[:, 2 * model_width:] + value_bias)).reshape(seq_rows, head_count, head_dim)
    scores = low_back(jnp.einsum('qhd,khd->hqk', queries, keys, precision=highest) + score_bias)
    scores = jnp.where(same_doc[None], scores, big_negative)
    lifted = jnp.exp(scores - lax.optimization_barrier(jnp.max(scores, axis=-1, keepdims=True)))
    probs = low(lifted / lax.optimization_barrier(jnp.sum(lifted, axis=-1, keepdims=True)))
    mixed = jnp.einsum('hqk,khd->qhd', probs, values, precision=highest).reshape(seq_rows, model_width)
    mixed = low(low_back(mixed))
    branch = low_back(product(mixed, out_weight) + out_bias)
    middle = layer_norm(hidden + branch, gain_one, shift_one)
    inner = low_back(product(low(middle), in_weight) + in_bias)
    active = low(jax.nn.gelu(inner, approximate=False))
    outer = low_back(product(active, back_weight) + back_bias)
    return layer_norm(middle + outer, gain_two, shift_two)

def reference(hidden_in, cotangent, lengths, coords, qkv_weight, query_bias, value_bias, out_weight, out_bias, norm1_gain, norm1_shift, in_weight, in_bias, back_weight, back_bias, norm2_gain, norm2_shift, line_table, horizontal_table, vertical_table):
    weight_list = tuple((item.astype(jnp.float32) for item in (qkv_weight, query_bias, value_bias, out_weight, out_bias, norm1_gain, norm1_shift, in_weight, in_bias, back_weight, back_bias, norm2_gain, norm2_shift)))
    table_list = tuple((item.astype(jnp.float32) for item in (line_table, horizontal_table, vertical_table)))
    model_width = hidden_in.shape[1]
    hidden = hidden_in.astype(jnp.float32).reshape(GROUPS, SEQ, model_width)
    place = jnp.arange(SEQ, dtype=jnp.int32)
    real_rows = (place[None, :] < lengths[:, None]).astype(jnp.float32)
    upstream = cotangent.astype(jnp.float32).reshape(GROUPS, SEQ, model_width) * real_rows[:, :, None]
    across = coords[0].reshape(GROUPS, SEQ)
    upward = coords[1].reshape(GROUPS, SEQ)

    def forward(hidden, weight_list, table_list):

        def one_group(item):
            group_rows, group_length, group_across, group_upward = item
            key_live = place < group_length
            same_doc = jnp.broadcast_to(key_live[None, :], (SEQ, SEQ))
            line_codes = bucket_of(place[None, :] - place[:, None], BUCKETS_1D, REACH_1D)
            across_codes = bucket_of(group_across[None, :] - group_across[:, None], BUCKETS_2D, REACH_2D)
            upward_codes = bucket_of(group_upward[None, :] - group_upward[:, None], BUCKETS_2D, REACH_2D)
            score_bias = (low(table_list[0])[line_codes] + low(table_list[1])[across_codes] + low(table_list[2])[upward_codes]).transpose(2, 0, 1)
            state = group_rows
            for layer_index in range(LAYERS):
                state = encoder_layer(state, tuple((item[layer_index] for item in weight_list)), score_bias, same_doc)
            return state
        return lax.map(jax.checkpoint(one_group), (hidden, lengths, across, upward))
    result, pull = jax.vjp(forward, hidden, weight_list, table_list)
    grad_hidden, grad_weights, grad_tables = pull(upstream)
    return (result.reshape(TOKENS, model_width).astype(jnp.bfloat16), grad_hidden.reshape(TOKENS, model_width).astype(jnp.bfloat16), grad_weights[0], grad_weights[1], grad_weights[2], grad_weights[3], grad_weights[4], grad_weights[5], grad_weights[6], grad_weights[7], grad_weights[8], grad_weights[9], grad_weights[10], grad_weights[11], grad_weights[12], grad_tables[0], grad_tables[1], grad_tables[2])
```

```python
import functools
import math

import jax
import jax.numpy as jnp
from jax import lax
from jax.experimental import pallas as pl
from jax.experimental.pallas import tpu as pltpu
from jax.sharding import PartitionSpec as P

REACH_1D = 128
REACH_2D = 256
COORD_TOP = 1000

eps_norm = 1e-12
big_negative = -1e30

BF = jnp.bfloat16
F4 = jnp.float32
AXES = ("dp", "blk")
VMEM = 56 * 1024 * 1024

HEAD = 64
QUAD = 256
LANES = 128


def bucket_marks(bucket_count, far_reach):
    half_count = bucket_count // 2
    exact_limit = half_count // 2
    thresholds = []
    for bucket_step in range(1, half_count):
        if bucket_step < exact_limit:
            thresholds.append(bucket_step)
        else:
            thresholds.append(
                math.ceil(
                    exact_limit
                    * (far_reach / exact_limit)
                    ** ((bucket_step - exact_limit) / (half_count - exact_limit))
                )
            )
    return thresholds


def params(**more):
    return pltpu.CompilerParams(vmem_limit_bytes=VMEM, **more)


def cost(flops, traffic):
    return pl.CostEstimate(flops=int(flops), bytes_accessed=int(traffic), transcendentals=0)


def mm(left, right):
    return jnp.dot(left, right, preferred_element_type=F4)


def mm_t(left, right):
    return lax.dot_general(left, right, (((1,), (1,)), ((), ())), preferred_element_type=F4)


def pick(table_row, codes):
    return jnp.take_along_axis(
        jnp.broadcast_to(table_row, codes.shape), codes, axis=1, mode="promise_in_bounds"
    )


def bias_kernel(heads, line_n, plane_n, scal, own_ref, keys_ref, plane_ref, line_ref, out_ref):
    rows = out_ref.shape[1]
    chunk = 32
    step = pl.program_id(0)
    length, half = scal[0], scal[1]
    magnitude = lax.broadcasted_iota(jnp.int32, (1, LANES), 1)

    def marks(base, count, reach):
        code = jnp.zeros((1, LANES), jnp.int32)
        for mark in bucket_marks(count, reach):
            code = code + (magnitude + base >= mark).astype(jnp.int32)
        return code

    near, far = marks(0, plane_n, REACH_2D), marks(LANES, plane_n, REACH_2D)
    flat = marks(0, line_n, REACH_1D)
    key_index = step * LANES + magnitude
    key_place = jnp.where(
        key_index < rows, half * rows + key_index, (1 - half) * rows + key_index - rows
    )
    live = key_place < length
    across_key, upward_key = keys_ref[0:1, :], keys_ref[1:2, :]

    def plane_code(offset):
        size = jnp.minimum(jnp.abs(offset), 2 * LANES - 1)
        low = jnp.bitwise_and(size, LANES - 1)
        code = jnp.where(size >= LANES, pick(far, low), pick(near, low))
        return code + jnp.where(offset > 0, plane_n // 2, 0)

    def body(index, carry):
        first = pl.multiple_of(index * chunk, chunk)
        span = pl.ds(first, chunk)
        across = plane_code(across_key - own_ref[span, 0:1])
        upward = plane_code(upward_key - own_ref[span, 1:2]) + plane_n
        place = (
            half * rows + first + lax.broadcasted_iota(jnp.int32, (chunk, LANES), 0)
        )
        offset = key_place - place
        along = pick(flat, jnp.minimum(jnp.abs(offset), LANES - 1)) + jnp.where(
            offset > 0, line_n // 2, 0
        )
        for head in range(heads):
            plane_row = plane_ref[head : head + 1, :]
            total = (
                pick(line_ref[head : head + 1, :], along)
                + pick(plane_row, across)
                + pick(plane_row, upward)
            )
            out_ref[head, span, :] = jnp.where(live, total, big_negative)
        return carry

    lax.fori_loop(0, rows // chunk, body, 0)


def score_biases(length, half, own_xy, key_xy, line_table, across_table, upward_table):
    heads = line_table.shape[1]
    rows, keys = own_xy.shape[1], key_xy.shape[1]
    line_n, plane_n = line_table.shape[0], across_table.shape[0]
    plane = jnp.concatenate([across_table, upward_table], axis=0).astype(F4).T
    line = jnp.pad(line_table.astype(F4).T, ((0, 0), (0, LANES - line_n)))
    whole = pl.BlockSpec(memory_space=pltpu.VMEM)
    return pl.pallas_call(
        functools.partial(bias_kernel, heads, line_n, plane_n),
        grid=(keys // LANES,),
        in_specs=[
            pl.BlockSpec(memory_space=pltpu.SMEM),
            whole,
            pl.BlockSpec((2, LANES), lambda j: (0, j)),
            whole,
            whole,
        ],
        out_specs=pl.BlockSpec((heads, rows, LANES), lambda j: (0, 0, j)),
        out_shape=jax.ShapeDtypeStruct((heads, rows, keys), F4),
        compiler_params=params(),
        cost_estimate=cost(3e9, heads * rows * keys * 4),
        name="score_bias",
    )(jnp.stack([length, half]), own_xy.T, key_xy, plane, line)


def head_masks(dtype):
    lane = lax.broadcasted_iota(jnp.int32, (1, QUAD), 1)
    return [
        ((lane >= h * HEAD) & (lane < (h + 1) * HEAD)).astype(dtype) for h in range(QUAD // HEAD)
    ]


def attn_fwd_kernel(x_ref, wq, wk, wv, bq, bv, bias_ref, q_out, k_out, v_out, p_out, o_out):
    rows = q_out.shape[0]
    x = x_ref[...]
    q = ((mm(x[:rows], wq[...]) + bq[...]) * 0.125).astype(BF)
    k = mm(x, wk[...]).astype(BF)
    v = (mm(x, wv[...]) + bv[...]).astype(BF)
    q_out[...] = q
    k_out[...] = k
    v_out[...] = v
    lane = lax.broadcasted_iota(jnp.int32, (rows, QUAD), 1)
    mixed = jnp.zeros((rows, QUAD), F4)
    for h, mask in enumerate(head_masks(BF)):
        s = mm_t(q * mask, k) + bias_ref[h]
        e = jnp.exp(s - jnp.max(s, axis=-1, keepdims=True))
        p = (e * (1.0 / jnp.sum(e, axis=-1, keepdims=True))).astype(BF)
        p_out[h] = p
        mixed = jnp.where(
            (lane >= h * HEAD) & (lane < (h + 1) * HEAD), mm(p, v), mixed
        )
    o_out[...] = mixed.astype(BF)


def attn_fwd(x_all, packed, bq, bv, bias):
    keys, width = x_all.shape
    heads, rows, _ = bias.shape
    quads = width // QUAD
    per = QUAD // HEAD
    weight = lambda base: pl.BlockSpec((width, QUAD), lambda j: (0, base * quads + j))
    vec = pl.BlockSpec((1, QUAD), lambda j: (0, j))
    cols = lambda n: pl.BlockSpec((n, QUAD), lambda j: (0, j))
    scores = pl.BlockSpec((per, rows, keys), lambda j: (j, 0, 0))
    sds = jax.ShapeDtypeStruct
    return pl.pallas_call(
        attn_fwd_kernel,
        grid=(quads,),
        in_specs=[
            pl.BlockSpec((keys, width), lambda j: (0, 0)),
            weight(0),
            weight(1),
            weight(2),
            vec,
            vec,
            scores,
        ],
        out_specs=[cols(rows), cols(keys), cols(keys), scores, cols(rows)],
        out_shape=[
            sds((rows, width), BF),
            sds((keys, width), BF),
            sds((keys, width), BF),
            sds((heads, rows, keys), BF),
            sds((rows, width), BF),
        ],
        compiler_params=params(),
        cost_estimate=cost(5e9, 16e6),
        name="attention_forward",
    )(x_all, packed, packed, packed, bq, bv, bias)


def normed(values):
    centered = values - jnp.mean(values, axis=-1, keepdims=True)
    variance = jnp.mean(centered * centered, axis=-1, keepdims=True)
    scale = lax.rsqrt(variance + eps_norm)
    return centered * scale, scale


def ffn_fwd_kernel(
    x_ref, o_ref, wo, win, wback, bo, g1, s1, bin_, bb, g2, s2,
    r1_out, h_out, act_out, slope_out, r2_out, x_out, low_out, middle, total,
):
    step = pl.program_id(0)

    @pl.when(step == 0)
    def _():
        r1 = x_ref[...].astype(F4) + mm(o_ref[...], wo[...]) + bo[...]
        r1_out[...] = r1
        n, _ = normed(r1)
        h = n * g1[...] + s1[...]
        middle[...] = h
        h_out[...] = h.astype(BF)
        total[...] = jnp.zeros_like(total)

    u = mm(h_out[...], win[...]) + bin_[...]
    cdf = 0.5 * (1.0 + lax.erf(u * 0.7071067811865476))
    act = (u * cdf).astype(BF)
    act_out[...] = act
    slope_out[...] = (cdf + u * (0.3989422804014327 * jnp.exp(-0.5 * u * u))).astype(BF)
    total[...] += mm(act, wback[...])

    @pl.when(step == pl.num_programs(0) - 1)
    def _():
        r2 = middle[...] + total[...] + bb[...]
        r2_out[...] = r2
        n, _ = normed(r2)
        x = n * g2[...] + s2[...]
        x_out[...] = x
        low_out[...] = x.astype(BF)


def ffn_fwd(x, o, packed, back, vecs):
    rows, width = x.shape
    ff = back.shape[0]
    parts = ff // width
    full = pl.BlockSpec((rows, width), lambda j: (0, 0))
    vec = pl.BlockSpec((1, width), lambda j: (0, 0))
    chunk = pl.BlockSpec((rows, width), lambda j: (0, j))
    sds = jax.ShapeDtypeStruct
    bo, g1, s1, bin_, bb, g2, s2 = vecs
    return pl.pallas_call(
        ffn_fwd_kernel,
        grid=(parts,),
        in_specs=[
            full,
            full,
            pl.BlockSpec((width, width), lambda j: (0, 3)),
            pl.BlockSpec((width, width), lambda j: (0, 4 + j)),
            pl.BlockSpec((width, width), lambda j: (j, 0)),
            vec, vec, vec,
            pl.BlockSpec((1, width), lambda j: (0, j)),
            vec, vec, vec,
        ],
        out_specs=[full, full, chunk, chunk, full, full, full],
        out_shape=[
            sds((rows, width), F4),
            sds((rows, width), BF),
            sds((rows, ff), BF),
            sds((rows, ff), BF),
            sds((rows, width), F4),
            sds((rows, width), F4),
            sds((rows, width), BF),
        ],
        scratch_shapes=[pltpu.VMEM((rows, width), F4), pltpu.VMEM((rows, width), F4)],
        compiler_params=params(),
        cost_estimate=cost(5e9, 20e6),
        name="dense_forward",
    )(x, o, packed, packed, back, bo, g1, s1, bin_, bb, g2, s2)


def norm_back(grad, values, gain):
    n, scale = normed(values)
    e = grad * gain
    inner = jnp.mean(e * n, axis=-1, keepdims=True)
    out = (e - jnp.mean(e, axis=-1, keepdims=True) - n * inner) * scale
    return out, jnp.sum(grad * n, axis=0, keepdims=True), jnp.sum(grad, axis=0, keepdims=True)


def ffn_bwd_kernel(
    own_ref, far_ref, r2_ref, g2, wback, slope, win, r1_ref, g1, wo,
    df_out, du_out, dr1_out, db_out, do_out, vec_out, binv_out, dr2, total,
):
    step = pl.program_id(0)

    @pl.when(step == 0)
    def _():
        grad = own_ref[...] + far_ref[...].astype(F4)
        out, gain, shift = norm_back(grad, r2_ref[...], g2[...])
        dr2[...] = out
        low = out.astype(BF)
        df_out[...] = low
        vec_out[3:4, :] = jnp.sum(low.astype(F4), axis=0, keepdims=True)
        vec_out[4:5, :] = gain
        vec_out[5:6, :] = shift
        total[...] = jnp.zeros_like(total)

    du = (mm_t(df_out[...], wback[...]) * slope[...].astype(F4)).astype(BF)
    du_out[...] = du
    binv_out[...] = jnp.sum(du.astype(F4), axis=0, keepdims=True)
    total[...] += mm_t(du, win[...])

    @pl.when(step == pl.num_programs(0) - 1)
    def _():
        out, gain, shift = norm_back(dr2[...] + total[...], r1_ref[...], g1[...])
        dr1_out[...] = out
        low = out.astype(BF)
        db_out[...] = low
        vec_out[0:1, :] = jnp.sum(low.astype(F4), axis=0, keepdims=True)
        vec_out[1:2, :] = gain
        vec_out[2:3, :] = shift
        do_out[...] = mm_t(low, wo[...]).astype(BF)


def ffn_bwd(own, far, r2, g2, back, slope, packed, r1, g1):
    rows, width = own.shape
    ff = back.shape[0]
    parts = ff // width
    full = pl.BlockSpec((rows, width), lambda j: (0, 0))
    vec = pl.BlockSpec((1, width), lambda j: (0, 0))
    chunk = pl.BlockSpec((rows, width), lambda j: (0, j))
    sds = jax.ShapeDtypeStruct
    return pl.pallas_call(
        ffn_bwd_kernel,
        grid=(parts,),
        in_specs=[
            full, full, full, vec,
            pl.BlockSpec((width, width), lambda j: (j, 0)),
            chunk,
            pl.BlockSpec((width, width), lambda j: (0, 4 + j)),
            full, vec,
            pl.BlockSpec((width, width), lambda j: (0, 3)),
        ],
        out_specs=[
            full, chunk, full, full, full,
            pl.BlockSpec((8, width), lambda j: (0, 0)),
            pl.BlockSpec((1, width), lambda j: (0, j)),
        ],
        out_shape=[
            sds((rows, width), BF),
            sds((rows, ff), BF),
            sds((rows, width), F4),
            sds((rows, width), BF),
            sds((rows, width), BF),
            sds((8, width), F4),
            sds((1, ff), F4),
        ],
        scratch_shapes=[pltpu.VMEM((rows, width), F4), pltpu.VMEM((rows, width), F4)],
        compiler_params=params(),
        cost_estimate=cost(5e9, 20e6),
        name="dense_backward",
    )(own, far, r2, g2, back, slope, packed, r1, g1, packed)


def attn_bwd_kernel(
    q_ref, k_ref, v_ref, p_ref, do_ref, wq, wk, wv, dr1_ref,
    dq_out, dk_out, dv_out, ds_out, own_out, far_out, vec_out, far_sum,
):
    step = pl.program_id(0)
    rows = q_ref.shape[0]

    @pl.when(step == 0)
    def _():
        own_out[...] = dr1_ref[...]
        far_sum[...] = jnp.zeros_like(far_sum)

    q, k, v, do = q_ref[...], k_ref[...], v_ref[...], do_ref[...]
    q_t, do_t = q.T, do.T
    lane = lax.broadcasted_iota(jnp.int32, (rows, QUAD), 1)
    dq = jnp.zeros((rows, QUAD), F4)
    dk_t, dv_t = [], []
    for h, mask in enumerate(head_masks(BF)):
        low = p_ref[h]
        p = low.astype(F4)
        t = p * mm_t(do * mask, v)
        ds = (t - p * jnp.sum(t, axis=-1, keepdims=True)).astype(BF)
        ds_out[h] = ds
        dq = jnp.where((lane >= h * HEAD) & (lane < (h + 1) * HEAD), mm(ds, k), dq)
        dk_t.append(mm(q_t[h * HEAD : (h + 1) * HEAD], ds))
        dv_t.append(mm(do_t[h * HEAD : (h + 1) * HEAD], low))
    dk = jnp.concatenate(dk_t, axis=0).T.astype(BF)
    dv = jnp.concatenate(dv_t, axis=0).T.astype(BF)
    dq = (dq.astype(BF).astype(F4) * 0.125).astype(BF)
    dq_out[...] = dq
    dk_out[...] = dk
    dv_out[...] = dv
    vec_out[0:1, :] = jnp.sum(dq.astype(F4), axis=0, keepdims=True)
    vec_out[1:2, :] = jnp.sum(dv.astype(F4), axis=0, keepdims=True)
    both = mm_t(dk, wk[...]) + mm_t(dv, wv[...])
    own_out[...] += mm_t(dq, wq[...]) + both[:rows]
    far_sum[...] += both[rows:]

    @pl.when(step == pl.num_programs(0) - 1)
    def _():
        far_out[...] = far_sum[...].astype(BF)


def attn_bwd(q, k, v, p, do, packed, dr1):
    heads, rows, keys = p.shape
    width = q.shape[1]
    quads = width // QUAD
    per = QUAD // HEAD
    weight = lambda base: pl.BlockSpec((width, QUAD), lambda j: (0, base * quads + j))
    cols = lambda n: pl.BlockSpec((n, QUAD), lambda j: (0, j))
    scores = pl.BlockSpec((per, rows, keys), lambda j: (j, 0, 0))
    full = pl.BlockSpec((rows, width), lambda j: (0, 0))
    sds = jax.ShapeDtypeStruct
    return pl.pallas_call(
        attn_bwd_kernel,
        grid=(quads,),
        in_specs=[
            cols(rows), cols(keys), cols(keys), scores, cols(rows),
            weight(0), weight(1), weight(2), full,
        ],
        out_specs=[
            cols(rows), cols(keys), cols(keys), scores, full, full,
            pl.BlockSpec((8, QUAD), lambda j: (0, j)),
        ],
        out_shape=[
            sds((rows, width), BF),
            sds((keys, width), BF),
            sds((keys, width), BF),
            sds((heads, rows, keys), BF),
            sds((rows, width), F4),
            sds((rows, width), BF),
            sds((8, width), F4),
        ],
        scratch_shapes=[pltpu.VMEM((rows, width), F4)],
        compiler_params=params(),
        cost_estimate=cost(8e9, 20e6),
        name="attention_backward",
    )(q, k, v, p, do, packed, packed, packed, dr1)


def wgrad_kernel(x_ref, dq, dk, dv, o_ref, db, h_ref, du, out_ref, x_t, h_t):
    step = pl.program_id(0)
    rows = o_ref.shape[0]

    @pl.when(step == 0)
    def _():
        x_t[...] = x_ref[...].T
        out_ref[...] = mm(x_t[:, :rows], dq[...]).astype(BF)

    @pl.when(step == 1)
    def _():
        out_ref[...] = mm(x_t[...], dk[...]).astype(BF)

    @pl.when(step == 2)
    def _():
        out_ref[...] = mm(x_t[...], dv[...]).astype(BF)

    @pl.when(step == 3)
    def _():
        h_t[...] = h_ref[...].T
        out_ref[...] = mm(o_ref[...].T, db[...]).astype(BF)

    @pl.when(step > 3)
    def _():
        out_ref[...] = mm(h_t[...], du[...]).astype(BF)


def wgrad(x_all, dq, dk, dv, o, db, h, du, columns):
    keys, width = x_all.shape
    rows, ff = du.shape
    parts = ff // width
    full = pl.BlockSpec((rows, width), lambda j: (0, 0))
    both = pl.BlockSpec((keys, width), lambda j: (0, 0))
    return pl.pallas_call(
        wgrad_kernel,
        grid=(4 + parts,),
        in_specs=[
            both, full, both, both, full, full, full,
            pl.BlockSpec((rows, width), lambda j: (0, jnp.maximum(j - 4, 0))),
        ],
        out_specs=pl.BlockSpec((width, width), lambda j: (0, j)),
        out_shape=jax.ShapeDtypeStruct((width, columns), BF),
        scratch_shapes=[pltpu.VMEM((width, keys), BF), pltpu.VMEM((width, rows), BF)],
        compiler_params=params(),
        cost_estimate=cost(4e9, 15e6),
        name="weight_gradients",
    )(x_all, dq, dk, dv, o, db, h, du)


def wgrad_back_kernel(own_rows, act, df, _, out_ref):
    width = df.shape[1]
    grad = mm(act[...].T, df[...])
    parts = out_ref.shape[1] // width
    grad = grad.reshape(grad.shape[0] // (own_rows * parts), parts, own_rows, width)
    for part in range(parts):
        out_ref[:, part * width : (part + 1) * width] = (
            grad[:, part].reshape(out_ref.shape[0], width).astype(BF)
        )


def wgrad_back(act, df, packed_grad, own_rows):
    rows, ff = act.shape
    width = df.shape[1]
    parts = ff // width
    return pl.pallas_call(
        functools.partial(wgrad_back_kernel, own_rows),
        grid=(parts,),
        in_specs=[
            pl.BlockSpec((rows, width), lambda j: (0, j)),
            pl.BlockSpec((rows, width), lambda j: (0, 0)),
            pl.BlockSpec(memory_space=pl.ANY),
        ],
        out_specs=pl.BlockSpec((width // parts, ff), lambda j: (j, 2)),
        out_shape=jax.ShapeDtypeStruct(packed_grad.shape, BF),
        input_output_aliases={2: 0},
        compiler_params=params(),
        cost_estimate=cost(2e9, 8e6),
        name="weight_gradients_back",
    )(act, df, packed_grad)


def edge_row(count, reach):
    half = count // 2
    marks = bucket_marks(count, reach)
    lane = lax.broadcasted_iota(jnp.int32, (1, LANES), 1)
    edges = jnp.full((1, LANES), -(1 << 20), jnp.int32)
    for k, mark in enumerate(marks):
        edges = jnp.where(lane == k, 1 - mark, edges)
        edges = jnp.where(lane == half - 1 + k, mark, edges)
    return jnp.where(lane == 2 * half - 2, 1 << 20, edges)


def tables_kernel(
    line_n, plane_n, keys_ref, own_ref, one_ref, two_ref, out_ref, steps, line_steps, spots
):
    keys, rows = keys_ref.shape[0], own_ref.shape[0]
    span = steps.shape[2]

    @pl.when(pl.program_id(0) == 0)
    def _():
        place = lax.broadcasted_iota(jnp.int32, (keys, span), 1)
        for plane in range(2):
            steps[plane] = (keys_ref[:, plane : plane + 1] < place).astype(F4).astype(BF)
            spots[plane] = jnp.clip(
                own_ref[:, plane : plane + 1] + edge_row(plane_n, REACH_2D), 0, COORD_TOP + 1
            )
        line_place = lax.broadcasted_iota(jnp.int32, (keys, keys), 1)
        line_steps[...] = (keys_ref[:, 2:3] <= line_place).astype(F4).astype(BF)
        spots[2] = jnp.clip(own_ref[:, 2:3] + edge_row(line_n, REACH_1D), 0, keys) - 1

    one, two = one_ref[0], two_ref[0]

    def collect(sums, spot):
        safe = jnp.maximum(spot, 0)
        low = jnp.bitwise_and(safe, LANES - 1)
        block = lax.shift_right_logical(safe, 7)
        found = jnp.zeros(spot.shape, F4)
        for b in range(sums.shape[1] // LANES):
            piece = jnp.take_along_axis(
                sums[:, b * LANES : (b + 1) * LANES], low, axis=1, mode="promise_in_bounds"
            )
            found = jnp.where(block == b, piece, found)
        return jnp.sum(jnp.where(spot >= 0, found, 0.0), axis=0, keepdims=True)

    for plane in range(2):
        sums = mm(one, steps[plane]) + mm(two, steps[plane])
        out_ref[0, plane : plane + 1, :] = collect(sums, spots[plane])
    sums = mm(one, line_steps[...]) + mm(two, line_steps[...])
    out_ref[0, 2:3, :] = collect(sums, spots[2])


def table_sums(key_columns, own_columns, one, two, line_n, plane_n):
    heads, rows, keys = one.shape
    span = -(-(COORD_TOP + 2) // LANES) * LANES
    whole = pl.BlockSpec(memory_space=pltpu.VMEM)
    scores = pl.BlockSpec((1, rows, keys), lambda j: (j, 0, 0))
    return pl.pallas_call(
        functools.partial(tables_kernel, line_n, plane_n),
        grid=(heads,),
        in_specs=[whole, whole, scores, scores],
        out_specs=pl.BlockSpec((1, 8, LANES), lambda j: (j, 0, 0)),
        out_shape=jax.ShapeDtypeStruct((heads, 8, LANES), F4),
        scratch_shapes=[
            pltpu.VMEM((2, keys, span), BF),
            pltpu.VMEM((keys, keys), BF),
            pltpu.VMEM((3, rows, LANES), jnp.int32),
        ],
        compiler_params=params(),
        cost_estimate=cost(16e9, 6e6),
        name="table_sums",
    )(key_columns, own_columns, one, two)


def buckets_from_sums(sums, count):
    half = count // 2
    below, above = sums[:, : half - 1], sums[:, half - 1 : 2 * half - 2]
    total = sums[:, 2 * half - 2 : 2 * half - 1]
    zero = jnp.zeros_like(total)
    lower = jnp.concatenate([above[:, :1], below], axis=1) - jnp.concatenate([below, zero], axis=1)
    upper = jnp.concatenate([above[:, 1:], total], axis=1) - above
    return jnp.concatenate([lower, zero, upper], axis=1).T


def exchange(block, devices, distance):
    return lax.ppermute(block, AXES, [(i, i ^ distance) for i in range(devices)])


def summed_everywhere(block, devices):
    distance = 1
    while distance < devices:
        block = block + exchange(block, devices, distance)
        distance *= 2
    return block


def on_device(
    devices,
    hidden_in, cotangent, lengths, coords,
    qkv_weight, query_bias, value_bias, out_weight, out_bias, norm1_gain, norm1_shift,
    in_weight, in_bias, back_weight, back_bias, norm2_gain, norm2_shift,
    line_table, horizontal_table, vertical_table,
):
    rows, width = hidden_in.shape
    layers, own_rows, _ = qkv_weight.shape
    ff = in_weight.shape[2]
    parts = ff // width
    line_n, plane_n = line_table.shape[0], horizontal_table.shape[0]
    half = lax.axis_index("blk")
    me = lax.axis_index(AXES)
    length = lengths[0]
    flip = lambda block: exchange(block, devices, 1)

    columns = 3 * width + width + 2 * ff
    vec_list = []
    for l in range(layers):
        vec_list += [query_bias[l], value_bias[l], out_bias[l], norm1_gain[l], norm1_shift[l]]
        vec_list += [in_bias[l, g * own_rows : (g + 1) * own_rows] for g in range(parts)]
        vec_list += [back_bias[l], norm2_gain[l], norm2_shift[l]]
    vec_count = len(vec_list) // layers
    vec_block = jnp.pad(jnp.stack(vec_list, axis=1), ((0, 0), (0, LANES - len(vec_list))))

    gathered = []
    for l in range(layers):
        pieces = [qkv_weight[l], out_weight[l], in_weight[l]]
        pieces += [back_weight[l, g * own_rows : (g + 1) * own_rows] for g in range(parts)]
        if l == 0:
            pieces.append(vec_block)
        gathered.append(
            lax.all_gather(jnp.concatenate(pieces, axis=1), AXES, axis=0, tiled=True)
        )

    far_x = flip(hidden_in)
    far_coords = flip(coords)
    key_coords = jnp.concatenate([coords, far_coords], axis=1)
    bias = score_biases(
        length, half, coords, key_coords, line_table, horizontal_table, vertical_table
    )

    vec_rows = gathered[0][:, columns : columns + len(vec_list)].astype(F4).T

    def vec_of(l, k):
        return vec_rows[l * vec_count + k][None, :]

    def in_bias_of(l):
        part = vec_rows[l * vec_count + 5 : l * vec_count + 5 + parts]
        return part.reshape(parts, devices, own_rows).transpose(1, 0, 2).reshape(1, ff)

    def back_of(l):
        part = gathered[l][:, columns - ff : columns].reshape(devices, own_rows, parts, width)
        return part.transpose(0, 2, 1, 3).reshape(ff, width)

    backs = [back_of(l) for l in range(layers)]
    state, low = hidden_in, hidden_in
    saved = []
    for l in range(layers):
        if l > 0:
            far_x = flip(low)
        x_all = jnp.concatenate([low, far_x], axis=0)
        q, k, v, p, o = attn_fwd(x_all, gathered[l], vec_of(l, 0), vec_of(l, 1), bias)
        r1, h, act, slope, r2, state, low = ffn_fwd(
            state, o, gathered[l], backs[l],
            (
                vec_of(l, 2), vec_of(l, 3), vec_of(l, 4), in_bias_of(l),
                vec_of(l, 5 + parts), vec_of(l, 6 + parts), vec_of(l, 7 + parts),
            ),
        )
        saved.append((x_all, q, k, v, p, o, r1, h, act, slope, r2))
    hidden_out = low

    place = half * rows + jnp.arange(rows, dtype=jnp.int32)
    own = jnp.where((place < length)[:, None], cotangent.astype(F4), 0.0)
    far = jnp.zeros((rows, width), BF)
    shards = [None] * layers
    vec_grads = [None] * layers
    score_grads = []
    for l in reversed(range(layers)):
        x_all, q, k, v, p, o, r1, h, act, slope, r2 = saved[l]
        df, du, dr1, db, do, vec_a, vec_in = ffn_bwd(
            own, far, r2, vec_of(l, 6 + parts), backs[l], slope, gathered[l], r1, vec_of(l, 3)
        )
        dq, dk, dv, ds, own, far_part, vec_b = attn_bwd(q, k, v, p, do, gathered[l], dr1)
        far = flip(far_part)
        packed = wgrad(x_all, dq, dk, dv, o, db, h, du, columns)
        packed = wgrad_back(act, df, packed, own_rows)
        shards[l] = lax.psum_scatter(packed, AXES, scatter_dimension=0, tiled=True).astype(F4)
        score_grads.append(ds)
        vec_grads[l] = jnp.concatenate(
            [vec_b[0:2], vec_a[0:3], vec_in.reshape(parts, width), vec_a[3:6]], axis=0
        )
    grad_in = (own + far.astype(F4)).astype(BF)

    other = (1 - half) * rows + jnp.arange(rows, dtype=jnp.int32)
    key_columns = jnp.concatenate(
        [key_coords, jnp.concatenate([place, other])[None]], axis=0
    ).T
    own_columns = jnp.concatenate([coords, place[None]], axis=0).T
    sums = table_sums(key_columns, own_columns, score_grads[0], score_grads[1], line_n, plane_n)
    heads = sums.shape[0]
    flat = jnp.concatenate(vec_grads + [sums[:, :3].reshape(-1, width)], axis=0)
    flat = summed_everywhere(flat, devices)
    sums = flat[layers * vec_count :].reshape(heads, 3, LANES)
    grad_across = buckets_from_sums(sums[:, 0], plane_n)
    grad_upward = buckets_from_sums(sums[:, 1], plane_n)
    grad_line = buckets_from_sums(sums[:, 2], line_n)

    vec_grad = flat[: layers * vec_count].reshape(layers, vec_count, width)
    mine = lax.dynamic_slice_in_dim(vec_grad, me * own_rows, own_rows, axis=2)
    wide = vec_grad[:, 5 : 5 + parts].reshape(layers, ff)
    grad_in_bias = lax.dynamic_slice_in_dim(wide, me * parts * own_rows, parts * own_rows, axis=1)
    rest = lambda k: mine[:, k]

    shard = jnp.stack(shards)
    grad_qkv = shard[:, :, : 3 * width]
    grad_out = shard[:, :, 3 * width : 4 * width]
    grad_inw = shard[:, :, 4 * width : 4 * width + ff]
    grad_back = (
        shard[:, :, 4 * width + ff :]
        .reshape(layers, own_rows, parts, width)
        .transpose(0, 2, 1, 3)
        .reshape(layers, parts * own_rows, width)
    )
    return (
        hidden_out, grad_in,
        grad_qkv, rest(0), rest(1), grad_out, rest(2), rest(3), rest(4),
        grad_inw, grad_in_bias, grad_back, rest(5 + parts), rest(6 + parts), rest(7 + parts),
        grad_line, grad_across, grad_upward,
    )


def solution(mesh):
    devices = mesh.shape["dp"] * mesh.shape["blk"]
    tokens = P(AXES, None)
    weight = P(None, AXES, None)
    vector = P(None, AXES)
    return jax.shard_map(
        functools.partial(on_device, devices),
        mesh=mesh,
        in_specs=(
            tokens, tokens, P("dp"), P(None, AXES),
            weight, vector, vector, weight, vector, vector, vector,
            weight, vector, weight, vector, vector, vector,
            P(), P(), P(),
        ),
        out_specs=(
            tokens, tokens,
            weight, vector, vector, weight, vector, vector, vector,
            weight, vector, weight, vector, vector, vector,
            P(), P(), P(),
        ),
        check_vma=False,
    )
```

```python
import functools
import math

import jax
import jax.numpy as jnp
from jax import lax
from jax.experimental import pallas as pl
from jax.experimental.pallas import tpu as pltpu
from jax.sharding import PartitionSpec as P

REACH_1D = 128
REACH_2D = 256
COORD_TOP = 1000

eps_norm = 1e-12
big_negative = -1e30

BF = jnp.bfloat16
F4 = jnp.float32
AXES = ("dp", "blk")
VMEM = 56 * 1024 * 1024

HEAD = 64
QUAD = 256
LANES = 128


def bucket_marks(bucket_count, far_reach):
    half_count = bucket_count // 2
    exact_limit = half_count // 2
    thresholds = []
    for bucket_step in range(1, half_count):
        if bucket_step < exact_limit:
            thresholds.append(bucket_step)
        else:
            thresholds.append(
                math.ceil(
                    exact_limit
                    * (far_reach / exact_limit)
                    ** ((bucket_step - exact_limit) / (half_count - exact_limit))
                )
            )
    return thresholds


def params(**more):
    return pltpu.CompilerParams(vmem_limit_bytes=VMEM, **more)


def cost(flops, traffic):
    return pl.CostEstimate(
        flops=int(flops / 20), bytes_accessed=int(traffic / 20), transcendentals=0
    )


def mm(left, right):
    return jnp.dot(left, right, preferred_element_type=F4)


def mm_t(left, right):
    return lax.dot_general(left, right, (((1,), (1,)), ((), ())), preferred_element_type=F4)


def over_rows(left, right):
    return lax.dot_general(left, right, (((0,), (0,)), ((), ())), preferred_element_type=F4)


def pick(table_row, codes):
    return jnp.take_along_axis(
        jnp.broadcast_to(table_row, codes.shape), codes, axis=1, mode="promise_in_bounds"
    )


def bias_kernel(heads, line_n, plane_n, scal, own_ref, keys_ref, plane_ref, line_ref, out_ref):
    rows = out_ref.shape[1]
    chunk = 32
    step = pl.program_id(0)
    length, half = scal[0], scal[1]
    magnitude = lax.broadcasted_iota(jnp.int32, (1, LANES), 1)

    def marks(base, count, reach):
        code = jnp.zeros((1, LANES), jnp.int32)
        for mark in bucket_marks(count, reach):
            code = code + (magnitude + base >= mark).astype(jnp.int32)
        return code

    near, far = marks(0, plane_n, REACH_2D), marks(LANES, plane_n, REACH_2D)
    flat = marks(0, line_n, REACH_1D)
    key_index = step * LANES + magnitude
    key_place = jnp.where(
        key_index < rows, half * rows + key_index, (1 - half) * rows + key_index - rows
    )
    live = key_place < length
    across_key, upward_key = keys_ref[0:1, :], keys_ref[1:2, :]

    def plane_code(offset):
        size = jnp.minimum(jnp.abs(offset), 2 * LANES - 1)
        low = jnp.bitwise_and(size, LANES - 1)
        code = jnp.where(size >= LANES, pick(far, low), pick(near, low))
        return code + jnp.where(offset > 0, plane_n // 2, 0)

    def body(index, carry):
        first = pl.multiple_of(index * chunk, chunk)
        span = pl.ds(first, chunk)
        across = plane_code(across_key - own_ref[span, 0:1])
        upward = plane_code(upward_key - own_ref[span, 1:2]) + plane_n
        place = (
            half * rows + first + lax.broadcasted_iota(jnp.int32, (chunk, LANES), 0)
        )
        offset = key_place - place
        along = pick(flat, jnp.minimum(jnp.abs(offset), LANES - 1)) + jnp.where(
            offset > 0, line_n // 2, 0
        )
        for head in range(heads):
            plane_row = plane_ref[head : head + 1, :]
            total = (
                pick(line_ref[head : head + 1, :], along)
                + pick(plane_row, across)
                + pick(plane_row, upward)
            )
            out_ref[head, span, :] = jnp.where(live, total, big_negative)
        return carry

    lax.fori_loop(0, rows // chunk, body, 0)


def score_biases(length, half, own_xy, key_xy, line_table, across_table, upward_table):
    heads = line_table.shape[1]
    rows, keys = own_xy.shape[1], key_xy.shape[1]
    line_n, plane_n = line_table.shape[0], across_table.shape[0]
    plane = jnp.concatenate([across_table, upward_table], axis=0).astype(F4).T
    line = jnp.pad(line_table.astype(F4).T, ((0, 0), (0, LANES - line_n)))
    whole = pl.BlockSpec(memory_space=pltpu.VMEM)
    return pl.pallas_call(
        functools.partial(bias_kernel, heads, line_n, plane_n),
        grid=(keys // LANES,),
        in_specs=[
            pl.BlockSpec(memory_space=pltpu.SMEM),
            whole,
            pl.BlockSpec((2, LANES), lambda j: (0, j)),
            whole,
            whole,
        ],
        out_specs=pl.BlockSpec((heads, rows, LANES), lambda j: (0, 0, j)),
        out_shape=jax.ShapeDtypeStruct((heads, rows, keys), F4),
        compiler_params=params(),
        cost_estimate=cost(3e9, heads * rows * keys * 4),
        name="score_bias",
    )(jnp.stack([length, half]), own_xy.T, key_xy, plane, line)


QUERY_BIAS, VALUE_BIAS, OUT_BIAS, GAIN_ONE, SHIFT_ONE, BACK_BIAS, GAIN_TWO, SHIFT_TWO = range(8)
VECS = 8
VEC_GRADS = 16


def pack_kernel(own_rows, qkv, out, inw, back, first, second, packed):
    layers, _, width = out.shape
    ff = inw.shape[2]
    base = 0
    for l in range(layers):
        if l == 0:
            first[...] = qkv[l, :, : 2 * width]
            second[:, :width] = qkv[l, :, 2 * width :]
            second[:, width:] = out[l]
        else:
            packed[:, base : base + 3 * width] = qkv[l]
            packed[:, base + 3 * width : base + 4 * width] = out[l]
            base += 4 * width
        packed[:, base : base + ff] = inw[l]
        base += ff
        wide = back[l].astype(F4)
        for g in range(ff // width):
            packed[:, base : base + width] = wide[g * own_rows : (g + 1) * own_rows].astype(BF)
            base += width


def pack(qkv, out, inw, back):
    layers, own_rows, width = out.shape
    ff = inw.shape[2]
    columns = (layers - 1) * 4 * width + layers * 2 * ff
    shape = lambda n: jax.ShapeDtypeStruct((own_rows, n), BF)
    return pl.pallas_call(
        functools.partial(pack_kernel, own_rows),
        out_shape=[shape(2 * width), shape(2 * width), shape(columns)],
        compiler_params=params(),
        name="pack_weights",
    )(qkv, out, inw, back)


class Weights:
    def __init__(self, layer, first, second, packed, parts):
        if layer == 0:
            self.q, self.k, self.v, self.o = (first, 0), (first, 1), (second, 0), (second, 1)
            base = 0
        else:
            base = 2 * parts + (layer - 1) * (4 + 2 * parts)
            self.q, self.k, self.v, self.o = [(packed, base + n) for n in range(4)]
            base += 4
        self.inw, self.back = (packed, base), (packed, base + parts)


def head_masks(dtype):
    lane = lax.broadcasted_iota(jnp.int32, (1, QUAD), 1)
    return [
        ((lane >= h * HEAD) & (lane < (h + 1) * HEAD)).astype(dtype) for h in range(QUAD // HEAD)
    ]


def attn_fwd_kernel(x_ref, wq, wk, wv, vec, bias_ref, q_out, k_out, v_out, p_out, o_out):
    rows = q_out.shape[0]
    x = x_ref[...]
    q = ((mm(x[:rows], wq[...]) + vec[QUERY_BIAS : QUERY_BIAS + 1]) * 0.125).astype(BF)
    k = mm(x, wk[...]).astype(BF)
    v = (mm(x, wv[...]) + vec[VALUE_BIAS : VALUE_BIAS + 1]).astype(BF)
    q_out[...] = q
    k_out[...] = k
    v_out[...] = v
    lane = lax.broadcasted_iota(jnp.int32, (rows, QUAD), 1)
    mixed = jnp.zeros((rows, QUAD), F4)
    for h, mask in enumerate(head_masks(BF)):
        s = mm_t(q * mask, k) + bias_ref[h]
        e = jnp.exp(s - jnp.max(s, axis=-1, keepdims=True))
        p = (e * (1.0 / jnp.sum(e, axis=-1, keepdims=True))).astype(BF)
        p_out[h] = p
        mixed = jnp.where((lane >= h * HEAD) & (lane < (h + 1) * HEAD), mm(p, v), mixed)
    o_out[...] = mixed.astype(BF)


def attn_fwd(layer, x_all, weights, vecs, bias):
    keys, width = x_all.shape
    heads, rows, _ = bias.shape
    quads = width // QUAD
    per = QUAD // HEAD
    weight = lambda place: pl.BlockSpec((width, QUAD), lambda j: (0, place[1] * quads + j))
    cols = lambda n: pl.BlockSpec((n, QUAD), lambda j: (0, j))
    scores = pl.BlockSpec((per, rows, keys), lambda j: (j, 0, 0))
    sds = jax.ShapeDtypeStruct
    return pl.pallas_call(
        attn_fwd_kernel,
        grid=(quads,),
        in_specs=[
            pl.BlockSpec((keys, width), lambda j: (0, 0)),
            weight(weights.q),
            weight(weights.k),
            weight(weights.v),
            pl.BlockSpec((VECS, QUAD), lambda j: (layer, j)),
            scores,
        ],
        out_specs=[cols(rows), cols(keys), cols(keys), scores, cols(rows)],
        out_shape=[
            sds((rows, width), BF),
            sds((keys, width), BF),
            sds((keys, width), BF),
            sds((heads, rows, keys), BF),
            sds((rows, width), BF),
        ],
        compiler_params=params(),
        cost_estimate=cost(8e9, 16e6),
        name="attention_forward",
    )(x_all, weights.q[0], weights.k[0], weights.v[0], vecs, bias)


def normed(values):
    centered = values - jnp.mean(values, axis=-1, keepdims=True)
    variance = jnp.mean(centered * centered, axis=-1, keepdims=True)
    scale = lax.rsqrt(variance + eps_norm)
    return centered * scale, scale


def natural_rows(own_rows, block, width):
    parts = block.shape[1] // width
    devices = block.shape[0] // own_rows
    wide = [
        block[:, g * width : (g + 1) * width].astype(F4).reshape(devices, 1, own_rows, width)
        for g in range(parts)
    ]
    return jnp.concatenate(wide, axis=1).reshape(devices * parts * own_rows, width).astype(BF)


def ffn_fwd_kernel(
    own_rows, x_ref, o_ref, wo, win, wback, vec, bin_,
    r1_out, h_out, act_out, slope_out, r2_out, x_out, low_out, middle, total,
):
    step = pl.program_id(0)
    width = x_ref.shape[1]
    row = lambda k: vec[k : k + 1]

    @pl.when(step == 0)
    def _():
        r1 = x_ref[...].astype(F4) + mm(o_ref[...], wo[...]) + row(OUT_BIAS)
        r1_out[...] = r1
        n, _ = normed(r1)
        h = n * row(GAIN_ONE) + row(SHIFT_ONE)
        middle[...] = h
        h_out[...] = h.astype(BF)
        total[...] = jnp.zeros_like(total)

    u = mm(h_out[...], win[...]) + bin_[...]
    cdf = 0.5 * (1.0 + lax.erf(u * 0.7071067811865476))
    act = (u * cdf).astype(BF)
    act_out[...] = act
    slope_out[...] = (cdf + u * (0.3989422804014327 * jnp.exp(-0.5 * u * u))).astype(BF)
    total[...] += mm(act, natural_rows(own_rows, wback[...], width))

    @pl.when(step == pl.num_programs(0) - 1)
    def _():
        r2 = middle[...] + total[...] + row(BACK_BIAS)
        r2_out[...] = r2
        n, _ = normed(r2)
        x = n * row(GAIN_TWO) + row(SHIFT_TWO)
        x_out[...] = x
        low_out[...] = x.astype(BF)


def ffn_fwd(layer, x, o, weights, vecs, in_biases, own_rows):
    rows, width = x.shape
    ff = in_biases.shape[1]
    parts = ff // width
    full = pl.BlockSpec((rows, width), lambda j: (0, 0))
    chunk = pl.BlockSpec((rows, width), lambda j: (0, j))
    sds = jax.ShapeDtypeStruct
    return pl.pallas_call(
        functools.partial(ffn_fwd_kernel, own_rows),
        grid=(parts,),
        in_specs=[
            full,
            full,
            pl.BlockSpec((width, width), lambda j: (0, weights.o[1])),
            pl.BlockSpec((width, width), lambda j: (0, weights.inw[1] + j)),
            pl.BlockSpec((width // parts, ff), lambda j: (j, weights.back[1] // parts)),
            pl.BlockSpec((VECS, width), lambda j: (layer, 0)),
            pl.BlockSpec((1, width), lambda j: (0, layer * parts + j)),
        ],
        out_specs=[full, full, chunk, chunk, full, full, full],
        out_shape=[
            sds((rows, width), F4),
            sds((rows, width), BF),
            sds((rows, ff), BF),
            sds((rows, ff), BF),
            sds((rows, width), F4),
            sds((rows, width), F4),
            sds((rows, width), BF),
        ],
        scratch_shapes=[pltpu.VMEM((rows, width), F4), pltpu.VMEM((rows, width), F4)],
        compiler_params=params(),
        cost_estimate=cost(9e9, 20e6),
        name="dense_forward",
    )(x, o, weights.o[0], weights.inw[0], weights.back[0], vecs, in_biases.reshape(1, -1))


def norm_back(grad, values, gain):
    n, scale = normed(values)
    e = grad * gain
    inner = jnp.mean(e * n, axis=-1, keepdims=True)
    out = (e - jnp.mean(e, axis=-1, keepdims=True) - n * inner) * scale
    return out, jnp.sum(grad * n, axis=0, keepdims=True), jnp.sum(grad, axis=0, keepdims=True)


def ffn_bwd_kernel(
    own_rows, own_ref, far_ref, r2_ref, vec, wback, slope, win, r1_ref, wo,
    joined, dr1_out, do_out, vec_out, dr2, total,
):
    step = pl.program_id(0)
    width = own_ref.shape[1]
    end = pl.num_programs(0) - 1
    ff = joined.shape[1] - 2 * width

    @pl.when(step == 0)
    def _():
        grad = own_ref[...] + far_ref[...].astype(F4)
        out, gain, shift = norm_back(grad, r2_ref[...], vec[GAIN_TWO : GAIN_TWO + 1])
        dr2[...] = out
        low = out.astype(BF)
        joined[:, ff : ff + width] = low
        vec_out[...] = jnp.zeros_like(vec_out)
        vec_out[3 + end + 1 : 3 + end + 2, :] = jnp.sum(low.astype(F4), axis=0, keepdims=True)
        vec_out[3 + end + 2 : 3 + end + 3, :] = gain
        vec_out[3 + end + 3 : 3 + end + 4, :] = shift
        total[...] = jnp.zeros_like(total)

    back = natural_rows(own_rows, wback[...], width)
    du = (mm_t(joined[:, ff : ff + width], back) * slope[...].astype(F4)).astype(BF)

    vec_out[pl.ds(3 + step, 1), :] = jnp.sum(du.astype(F4), axis=0, keepdims=True)

    joined[:, pl.ds(pl.multiple_of(step * width, width), width)] = du
    total[...] += mm_t(du, win[...])

    @pl.when(step == pl.num_programs(0) - 1)
    def _():
        out, gain, shift = norm_back(
            dr2[...] + total[...], r1_ref[...], vec[GAIN_ONE : GAIN_ONE + 1]
        )
        dr1_out[...] = out
        low = out.astype(BF)
        joined[:, ff + width :] = low
        vec_out[0:1, :] = jnp.sum(low.astype(F4), axis=0, keepdims=True)
        vec_out[1:2, :] = gain
        vec_out[2:3, :] = shift
        do_out[...] = mm_t(low, wo[...]).astype(BF)


def ffn_bwd(layer, own, far, r2, vecs, slope, weights, r1, own_rows):
    rows, width = own.shape
    ff = slope.shape[1]
    parts = ff // width
    full = pl.BlockSpec((rows, width), lambda j: (0, 0))
    chunk = pl.BlockSpec((rows, width), lambda j: (0, j))
    sds = jax.ShapeDtypeStruct
    return pl.pallas_call(
        functools.partial(ffn_bwd_kernel, own_rows),
        grid=(parts,),
        in_specs=[
            full, full, full,
            pl.BlockSpec((VECS, width), lambda j: (layer, 0)),
            pl.BlockSpec((width // parts, ff), lambda j: (j, weights.back[1] // parts)),
            chunk,
            pl.BlockSpec((width, width), lambda j: (0, weights.inw[1] + j)),
            full,
            pl.BlockSpec((width, width), lambda j: (0, weights.o[1])),
        ],
        out_specs=[
            pl.BlockSpec((rows, ff + 2 * width), lambda j: (0, 0)),
            full, full,
            pl.BlockSpec((VEC_GRADS, width), lambda j: (0, 0)),
        ],
        out_shape=[
            sds((rows, ff + 2 * width), BF),
            sds((rows, width), F4),
            sds((rows, width), BF),
            sds((VEC_GRADS, width), F4),
        ],
        scratch_shapes=[pltpu.VMEM((rows, width), F4), pltpu.VMEM((rows, width), F4)],
        compiler_params=params(),
        cost_estimate=cost(9e9, 20e6),
        name="dense_backward",
    )(own, far, r2, vecs, weights.back[0], slope, weights.inw[0], r1, weights.o[0])


def attn_bwd_kernel(
    q_ref, k_ref, v_ref, p_ref, do_ref, wq, wk, wv, dr1_ref, vec_ref,
    joined, ds_out, own_out, far_out, vec_out, far_sum,
):
    step = pl.program_id(0)
    rows = q_ref.shape[0]

    @pl.when(step == 0)
    def _():
        own_out[...] = dr1_ref[...]
        far_sum[...] = jnp.zeros_like(far_sum)

    q, k, v, do = q_ref[...], k_ref[...], v_ref[...], do_ref[...]
    q_t, do_t = q.T, do.T
    lane = lax.broadcasted_iota(jnp.int32, (rows, QUAD), 1)
    dq = jnp.zeros((rows, QUAD), F4)
    dk_t, dv_t = [], []
    for h, mask in enumerate(head_masks(BF)):
        low = p_ref[h]
        p = low.astype(F4)
        t = p * mm_t(do * mask, v)
        ds = (t - p * jnp.sum(t, axis=-1, keepdims=True)).astype(BF)
        ds_out[h] = ds
        dq = jnp.where((lane >= h * HEAD) & (lane < (h + 1) * HEAD), mm(ds, k), dq)
        dk_t.append(mm(q_t[h * HEAD : (h + 1) * HEAD], ds))
        dv_t.append(mm(do_t[h * HEAD : (h + 1) * HEAD], low))
    dk = jnp.concatenate(dk_t, axis=0).T.astype(BF)
    dv = jnp.concatenate(dv_t, axis=0).T.astype(BF)
    dq = (dq.astype(BF).astype(F4) * 0.125).astype(BF)
    keys = k.shape[0]
    joined[:keys] = dk
    joined[keys : 2 * keys] = dv
    joined[2 * keys :] = dq
    vec_out[: VEC_GRADS - 2] = vec_ref[: VEC_GRADS - 2]
    vec_out[VEC_GRADS - 2 : VEC_GRADS - 1] = jnp.sum(dq.astype(F4), axis=0, keepdims=True)
    vec_out[VEC_GRADS - 1 :] = jnp.sum(dv.astype(F4), axis=0, keepdims=True)
    both = mm_t(dk, wk[...]) + mm_t(dv, wv[...])
    own_out[...] += mm_t(dq, wq[...]) + both[:rows]
    far_sum[...] += both[rows:]

    @pl.when(step == pl.num_programs(0) - 1)
    def _():
        far_out[...] = far_sum[...].astype(BF)


def attn_bwd(q, k, v, p, do, weights, dr1, vec):
    heads, rows, keys = p.shape
    width = q.shape[1]
    quads = width // QUAD
    per = QUAD // HEAD
    weight = lambda place: pl.BlockSpec((width, QUAD), lambda j: (0, place[1] * quads + j))
    cols = lambda n: pl.BlockSpec((n, QUAD), lambda j: (0, j))
    scores = pl.BlockSpec((per, rows, keys), lambda j: (j, 0, 0))
    full = pl.BlockSpec((rows, width), lambda j: (0, 0))
    sds = jax.ShapeDtypeStruct
    return pl.pallas_call(
        attn_bwd_kernel,
        grid=(quads,),
        in_specs=[
            cols(rows), cols(keys), cols(keys), scores, cols(rows),
            weight(weights.q), weight(weights.k), weight(weights.v), full,
            cols(VEC_GRADS),
        ],
        out_specs=[
            cols(2 * keys + rows), scores, full, full,
            cols(VEC_GRADS),
        ],
        out_shape=[
            sds((2 * keys + rows, width), BF),
            sds((heads, rows, keys), BF),
            sds((rows, width), F4),
            sds((rows, width), BF),
            sds((VEC_GRADS, width), F4),
        ],
        scratch_shapes=[pltpu.VMEM((rows, width), F4)],
        compiler_params=params(),
        cost_estimate=cost(10e9, 20e6),
        name="attention_backward",
    )(q, k, v, p, do, weights.q[0], weights.k[0], weights.v[0], dr1, vec)


CORE, SIDE_X, SIDE_Y, TOP = 2, 1, 4, 8
EVERY = slice(None)


def core_rows(pos, block, group_rows):
    block = block.reshape(block.shape[0] // (2 * group_rows), 2, group_rows, block.shape[1])
    return jnp.where(pos[0] == 0, block[:, 0], block[:, 1]).reshape(-1, block.shape[3])


def part_along(first, grad, own_rows):
    inner = own_rows if first == SIDE_X else 2 * own_rows
    grad = grad.reshape(grad.shape[0] // (2 * inner), 2, inner, grad.shape[1])
    return grad[:, 0].reshape(-1, grad.shape[3]), grad[:, 1].reshape(-1, grad.shape[3])


def put(first, pos, zero, one, outs, where=(EVERY, EVERY)):
    low = pos[1 if first == SIDE_X else 2] == 0
    outs[0][where] = jnp.where(low, zero, one).astype(BF)
    outs[1][where] = jnp.where(low, one, zero).astype(BF)


def attn_pair_kernel(own_rows, pos, x_a, g_a, o_a, e_a, x_b, g_b, o_b, e_b,
                     keep, send, keep_too, send_too, t_a, t_b):
    step = pl.program_id(0)
    rows, keys = o_a.shape[0], x_a.shape[0]

    def emit(grad, first=SIDE_X, outs=(keep, send)):
        put(first, pos, *part_along(first, grad, own_rows), outs)

    @pl.when(step == 0)
    def _():
        t_a[...] = core_rows(pos, x_a[...].T, 2 * own_rows)
        t_b[...] = core_rows(pos, x_b[...].T, 2 * own_rows)
        emit(mm(t_a[:, :rows], g_a[2 * keys :]) + mm(t_b[:, :rows], g_b[2 * keys :]))

    @pl.when(step == 1)
    def _():
        emit(mm(t_a[...], g_a[:keys]) + mm(t_b[...], g_b[:keys]))

    @pl.when(step == 2)
    def _():
        emit(mm(t_a[...], g_a[keys : 2 * keys]) + mm(t_b[...], g_b[keys : 2 * keys]), SIDE_Y, (keep_too, send_too))

    @pl.when(step == 3)
    def _():
        left = core_rows(pos, o_a[...].T, 2 * own_rows)
        right = core_rows(pos, o_b[...].T, 2 * own_rows)
        emit(mm(left, e_a[...]) + mm(right, e_b[...]), SIDE_Y, (keep_too, send_too))


def in_pair_kernel(own_rows, pos, h_a, u_a, h_b, u_b, _, __, keep, send, t_a, t_b):
    @pl.when(pl.program_id(0) == 0)
    def _():
        t_a[...] = core_rows(pos, h_a[...].T, 2 * own_rows)
        t_b[...] = core_rows(pos, h_b[...].T, 2 * own_rows)

    grad = mm(t_a[...], u_a[...]) + mm(t_b[...], u_b[...])
    put(SIDE_X, pos, *part_along(SIDE_X, grad, own_rows), (keep, send))


def back_pair_kernel(own_rows, pos, f_a, a_a, f_b, a_b, _, __, keep, send):
    width = f_a.shape[1]
    parts = keep.shape[1] // width
    inner = 2 * parts * own_rows
    grad = mm(core_rows(pos, a_a[...].T, inner), f_a[...]) + mm(
        core_rows(pos, a_b[...].T, inner), f_b[...]
    )
    grad = grad.reshape(2, 2, parts, own_rows, width)
    for g in range(parts):
        zero = grad[0, :, g].reshape(2 * own_rows, width)
        one = grad[1, :, g].reshape(2 * own_rows, width)
        put(SIDE_Y, pos, zero, one, (keep, send), (EVERY, slice(g * width, (g + 1) * width)))


def attn_pair(pos, own_rows, mine, theirs, columns):
    keys, width = mine[0].shape
    rows, last = mine[3].shape
    base = columns // width - 2
    whole = lambda block: pl.BlockSpec(block.shape, lambda j: (0, 0))
    turned = pltpu.VMEM((width // 2, keys), BF)
    specs = [whole(block) for block in mine[:3]]
    specs.append(pl.BlockSpec((rows, width), lambda j: (0, last // width - 1)))
    early = pl.BlockSpec((width // 4, width), lambda j: (0, base + jnp.minimum(j, 1)))
    late = pl.BlockSpec((width // 4, width), lambda j: (0, base + jnp.maximum(j - 2, 0)))
    return pl.pallas_call(
        functools.partial(attn_pair_kernel, own_rows),
        grid=(4,),
        in_specs=[pl.BlockSpec(memory_space=pltpu.SMEM)] + specs * 2,
        out_specs=[early, early, late, late],
        out_shape=[jax.ShapeDtypeStruct((width // 4, columns), BF)] * 4,
        scratch_shapes=[turned, turned],
        compiler_params=params(),
        cost_estimate=cost(4e9, 8e6),
        name="attention_weight_gradients",
    )(pos, *mine, *theirs)


def pair_call(body, pos, arrays, specs, grid, group, out_spec, scratch, name):
    anywhere = pl.BlockSpec(memory_space=pl.ANY)
    first = 1 + len(arrays)
    return pl.pallas_call(
        body,
        grid=grid,
        in_specs=[pl.BlockSpec(memory_space=pltpu.SMEM)] + specs + [anywhere] * 2,
        out_specs=[out_spec] * 2,
        out_shape=[jax.ShapeDtypeStruct(block.shape, block.dtype) for block in group],
        input_output_aliases={first: 0, first + 1: 1},
        scratch_shapes=scratch,
        compiler_params=params(),
        cost_estimate=cost(4e9, 8e6),
        name=name,
    )(pos, *arrays, *group)


def in_pair(pos, own_rows, mine, theirs, group):
    rows, width = mine[0].shape
    full = pl.BlockSpec((rows, width), lambda j: (0, 0))
    chunk = pl.BlockSpec((rows, width), lambda j: (0, j))
    turned = pltpu.VMEM((width // 2, rows), BF)
    return pair_call(
        functools.partial(in_pair_kernel, own_rows), pos, [*mine, *theirs],
        [full, chunk] * 2, (mine[1].shape[1] // width - 2,), group,
        pl.BlockSpec((width // 4, width), lambda j: (0, j)), [turned, turned],
        "in_weight_gradients",
    )


def back_pair(pos, own_rows, mine, theirs, group):
    rows, ff = mine[1].shape
    width = (mine[0].shape[1] - ff) // 2
    full = pl.BlockSpec((rows, width), lambda j: (0, ff // width))
    tops = width // (TOP * own_rows)
    chunk = pl.BlockSpec((rows, ff // tops), lambda j: (0, j))
    return pair_call(
        functools.partial(back_pair_kernel, own_rows), pos, [*mine, *theirs],
        [full, chunk] * 2, (tops,), group,
        pl.BlockSpec((width // (4 * tops), ff), lambda j: (j, 0)), [],
        "back_weight_gradients",
    )


def cut(total, index, inner):
    total = total.reshape(total.shape[0] // (2 * inner), 2, inner, total.shape[1])
    pick_one = lambda i: lax.dynamic_index_in_dim(total, i, 1, keepdims=False)
    return [pick_one(i).reshape(-1, total.shape[3]) for i in (index, 1 - index)]


def fold(keep, came, index, inner):
    k, s = cut(keep, index, inner), cut(came, index, inner)
    return [(a.astype(F4) + b.astype(F4)).astype(BF) for a, b in zip(k, s)]


class Sum:
    def __init__(self, devices, me, own_rows, order, axes, pair):
        tops, top = [], TOP
        while top < devices:
            tops.append(top)
            top *= 2
        self.axes = list(axes) + tops
        self.devices, self.me, self.own_rows, self.order = devices, me, own_rows, order
        self.send(*pair)

    def send(self, keep, send):
        self.keep = keep
        self.came = exchange(send, self.devices, self.axes.pop(0))

    def turn(self):
        axis = self.axes[0]
        inner = self.own_rows * (2 if axis == SIDE_Y and SIDE_X in self.axes else 1)
        index = jnp.bitwise_and(self.me // axis, 1)
        self.send(*self.order(lambda k, c: fold(k, c, index, inner), self.keep, self.came))

    def total(self):
        return self.keep.astype(F4) + self.came.astype(F4)


class Together:
    def __init__(self, joined, *groups):
        self.joined, self.groups = joined, groups
        self.axes, self.devices, self.me = groups[0].axes, groups[0].devices, groups[0].me
        self.own_rows, self.order = groups[0].own_rows, groups[0].order
        self.keep = None

    def turn(self, *also):
        axis = self.axes.pop(0)
        index = jnp.bitwise_and(self.me // axis, 1)

        def halved(keep, came):
            total = keep.astype(F4) + came.astype(F4)
            count, rows, columns = total.shape
            total = total.reshape(count, rows // (2 * self.own_rows), 2, self.own_rows, columns)
            one = lambda i: lax.dynamic_index_in_dim(total, i, 2, keepdims=False)
            shape = (count, rows // 2, columns)
            return [one(i).reshape(shape).astype(BF) for i in (index, 1 - index)]

        if self.keep is None:
            keep, send = self.order(
                lambda keeps, cames, *_: halved(self.joined(keeps), self.joined(cames)),
                [g.keep for g in self.groups], [g.came for g in self.groups], *also,
            )
        else:
            keep, send = self.order(lambda k, c, *_: halved(k, c), self.keep, self.came, *also)
        self.keep, self.came = keep, exchange(send, self.devices, axis)

    def totals(self):
        return list(self.keep.astype(F4) + self.came.astype(F4))


class Everywhere:
    def __init__(self, devices, order, block):
        tops, top = [], TOP
        while top < devices:
            tops.append(top)
            top *= 2
        self.axes = [CORE] + tops + [SIDE_X, SIDE_Y]
        self.devices, self.order = devices, order
        self.send(block)

    def send(self, block):
        self.block, self.came = block, exchange(block, self.devices, self.axes.pop(0))

    def step(self):
        self.send(self.order(lambda b, c: b + c, self.block, self.came))

    def total(self):
        return self.block + self.came


class Order:
    def __init__(self):
        self.last = None

    def __call__(self, call, *arrays):
        if self.last is not None:
            arrays, _ = lax.optimization_barrier((arrays, self.last))
        out = call(*arrays)
        self.last = jax.tree.leaves(out)[0]
        return out


def edge_row(count, reach):
    half = count // 2
    marks = bucket_marks(count, reach)
    lane = lax.broadcasted_iota(jnp.int32, (1, LANES), 1)
    edges = jnp.full((1, LANES), -(1 << 20), jnp.int32)
    for k, mark in enumerate(marks):
        edges = jnp.where(lane == k, 1 - mark, edges)
        edges = jnp.where(lane == half - 1 + k, mark, edges)
    return jnp.where(lane == 2 * half - 2, 1 << 20, edges)


def tables_kernel(
    line_n, plane_n, keys_ref, own_ref, one_ref, two_ref, out_ref, steps, line_steps, spots
):
    keys, rows = keys_ref.shape[0], own_ref.shape[0]
    span = steps.shape[2]

    @pl.when(pl.program_id(0) == 0)
    def _():
        place = lax.broadcasted_iota(jnp.int32, (keys, span), 1)
        for plane in range(2):
            steps[plane] = (keys_ref[:, plane : plane + 1] < place).astype(F4).astype(BF)
            spots[plane] = jnp.clip(
                own_ref[:, plane : plane + 1] + edge_row(plane_n, REACH_2D), 0, COORD_TOP + 1
            )
        line_place = lax.broadcasted_iota(jnp.int32, (keys, keys), 1)
        line_steps[...] = (keys_ref[:, 2:3] <= line_place).astype(F4).astype(BF)
        spots[2] = jnp.clip(own_ref[:, 2:3] + edge_row(line_n, REACH_1D), 0, keys) - 1

    one, two = one_ref[0], two_ref[0]

    def collect(sums, spot):
        safe = jnp.maximum(spot, 0)
        low = jnp.bitwise_and(safe, LANES - 1)
        block = lax.shift_right_logical(safe, 7)
        found = jnp.zeros(spot.shape, F4)
        for b in range(sums.shape[1] // LANES):
            piece = jnp.take_along_axis(
                sums[:, b * LANES : (b + 1) * LANES], low, axis=1, mode="promise_in_bounds"
            )
            found = jnp.where(block == b, piece, found)
        return jnp.sum(jnp.where(spot >= 0, found, 0.0), axis=0, keepdims=True)

    for plane in range(2):
        sums = mm(one, steps[plane]) + mm(two, steps[plane])
        out_ref[0, plane : plane + 1, :] = collect(sums, spots[plane])
    sums = mm(one, line_steps[...]) + mm(two, line_steps[...])
    out_ref[0, 2:3, :] = collect(sums, spots[2])


def table_sums(key_columns, own_columns, one, two, line_n, plane_n):
    heads, rows, keys = one.shape
    span = -(-(COORD_TOP + 2) // LANES) * LANES
    whole = pl.BlockSpec(memory_space=pltpu.VMEM)
    scores = pl.BlockSpec((1, rows, keys), lambda j: (j, 0, 0))
    return pl.pallas_call(
        functools.partial(tables_kernel, line_n, plane_n),
        grid=(heads,),
        in_specs=[whole, whole, scores, scores],
        out_specs=pl.BlockSpec((1, 8, LANES), lambda j: (j, 0, 0)),
        out_shape=jax.ShapeDtypeStruct((heads, 8, LANES), F4),
        scratch_shapes=[
            pltpu.VMEM((2, keys, span), BF),
            pltpu.VMEM((keys, keys), BF),
            pltpu.VMEM((3, rows, LANES), jnp.int32),
        ],
        compiler_params=params(),
        cost_estimate=cost(16e9, 6e6),
        name="table_sums",
    )(key_columns, own_columns, one, two)


def buckets_from_sums(sums, count):
    half = count // 2
    below, above = sums[:, : half - 1], sums[:, half - 1 : 2 * half - 2]
    total = sums[:, 2 * half - 2 : 2 * half - 1]
    zero = jnp.zeros_like(total)
    lower = jnp.concatenate([above[:, :1], below], axis=1) - jnp.concatenate([below, zero], axis=1)
    upper = jnp.concatenate([above[:, 1:], total], axis=1) - above
    return jnp.concatenate([lower, zero, upper], axis=1).T


def exchange(block, devices, distance):
    return lax.ppermute(block, AXES, [(i, i ^ distance) for i in range(devices)])


def summed_everywhere(block, devices):
    distance = 1
    while distance < devices:
        block = block + exchange(block, devices, distance)
        distance *= 2
    return block


def all_rows(block, devices, me, axes):
    rows, columns = block.shape
    block = block[None]
    had = []
    for axis in axes:
        came = exchange(block, devices, axis)
        upper = jnp.bitwise_and(me // axis, 1) == 1
        inner = 1
        for other in had:
            inner *= 2 if other < axis else 1
        shape = (block.shape[0] // inner, 1, inner, rows, columns)
        mine, theirs = block.reshape(shape), came.reshape(shape)
        block = jnp.where(
            upper,
            jnp.concatenate([theirs, mine], axis=1),
            jnp.concatenate([mine, theirs], axis=1),
        ).reshape(-1, rows, columns)
        had.append(axis)
    return block.reshape(-1, columns)


def gathered_small(block, devices, me):
    count = 1
    block = block[None]
    while count < devices:
        came = exchange(block, devices, count)
        upper = jnp.bitwise_and(me // count, 1) == 1
        block = jnp.concatenate(
            [jnp.where(upper, came, block), jnp.where(upper, block, came)], axis=0
        )
        count *= 2
    return block


def on_device(
    devices,
    hidden_in, cotangent, lengths, coords,
    qkv_weight, query_bias, value_bias, out_weight, out_bias, norm1_gain, norm1_shift,
    in_weight, in_bias, back_weight, back_bias, norm2_gain, norm2_shift,
    line_table, horizontal_table, vertical_table,
):
    rows, width = hidden_in.shape
    layers, own_rows, _ = qkv_weight.shape
    ff = in_weight.shape[2]
    parts = ff // width
    line_n, plane_n = line_table.shape[0], horizontal_table.shape[0]
    half = lax.axis_index("blk")
    me = lax.axis_index(AXES)
    length = lengths[0]
    flip = lambda block: exchange(block, devices, 1)
    split = own_rows % 8 == 0

    first, second, packed = pack(qkv_weight, out_weight, in_weight, back_weight)
    packed = lax.all_gather(packed, AXES, axis=0, tiled=True)
    if split:
        tops = [top for top in (TOP << n for n in range(devices)) if top < devices][::-1]
        first = all_rows(first, devices, me, tops + [SIDE_Y, SIDE_X, CORE])
        second = all_rows(second, devices, me, tops + [SIDE_X, SIDE_Y, CORE])
    else:
        first = lax.all_gather(first, AXES, axis=0, tiled=True)
        second = lax.all_gather(second, AXES, axis=0, tiled=True)
    far_x = flip(hidden_in)
    far_coords = flip(coords)
    vec_local = jnp.stack(
        [query_bias, value_bias, out_bias, norm1_gain, norm1_shift, back_bias, norm2_gain,
         norm2_shift], axis=1,
    ).reshape(layers * VECS, own_rows)
    in_local = in_bias.reshape(layers * parts, own_rows)
    small = gathered_small(
        jnp.concatenate([vec_local, in_local], axis=0).astype(F4), devices, me
    )
    vecs = small[:, : layers * VECS].transpose(1, 0, 2).reshape(layers * VECS, width)
    in_biases = (
        small[:, layers * VECS :]
        .reshape(devices, layers, parts * own_rows)
        .transpose(1, 0, 2)
        .reshape(layers, ff)
    )
    key_coords = jnp.concatenate([coords, far_coords], axis=1)
    bias = score_biases(
        length, half, coords, key_coords, line_table, horizontal_table, vertical_table
    )

    weights = [Weights(l, first, second, packed, parts) for l in range(layers)]
    state, low = hidden_in, hidden_in
    saved, kept = [], []
    for l in range(layers):
        if l > 0:
            far_x = flip(low)
        if kept:
            far_x, *kept[-1] = lax.optimization_barrier((far_x, *kept[-1]))
        x_all = jnp.concatenate([low, far_x], axis=0)
        q, k, v, p, o = attn_fwd(l, x_all, weights[l], vecs, bias)
        r1, h, act, slope, r2, state, low = ffn_fwd(
            l, state, o, weights[l], vecs, in_biases, own_rows
        )
        saved.append((x_all, q, k, v, p, o, r1, h, act, slope, r2))
        if split:
            kept.append([exchange(block, devices, CORE) for block in (x_all, o, h, act)])
    hidden_out = low

    place = half * rows + jnp.arange(rows, dtype=jnp.int32)
    other = (1 - half) * rows + jnp.arange(rows, dtype=jnp.int32)
    key_columns = jnp.concatenate(
        [key_coords, jnp.concatenate([place, other])[None]], axis=0
    ).T
    own_columns = jnp.concatenate([coords, place[None]], axis=0).T
    own = jnp.where((place < length)[:, None], cotangent.astype(F4), 0.0)
    far = jnp.zeros((rows, width), BF)
    bit = lambda mask: jnp.bitwise_and(me // mask, 1).astype(jnp.int32)
    pos = jnp.stack([bit(CORE), bit(SIDE_X), bit(SIDE_Y)])
    top = (me // TOP).astype(jnp.int32)
    vec_grads = [None] * layers
    score_grads = [None] * layers
    order = Order()
    swap = lambda block: exchange(block, devices, CORE)
    begin = lambda axes, pair: Sum(devices, me, own_rows, order, axes, pair)

    def dense_part(l, own, far, *also):
        r2, r1, slope = saved[l][10], saved[l][6], saved[l][9]
        return order(
            lambda own, far, *_: ffn_bwd(l, own, far, r2, vecs, slope, weights[l], r1, own_rows),
            own, far, *also,
        )

    def attn_part(l, do, dr1, vec, *also):
        q, k, v, p = saved[l][1:5]
        out = order(
            lambda do, dr1, vec, *_: attn_bwd(q, k, v, p, do, weights[l], dr1, vec),
            do, dr1, vec, *also,
        )
        *out, score_grads[l], own, far_part, vec_grads[l] = out
        return *out, own, far_part

    shards = [None] * layers
    if split:

        def attn_grads(l, dense, dense_b, joined, joined_b):
            x_b, o_b = kept[l][:2]
            out = order(
                lambda *a: attn_pair(pos, own_rows, a[:4], a[4:], ff + 2 * width),
                saved[l][0], joined, saved[l][5], dense, x_b, joined_b, o_b, dense_b,
            )
            return out[:2], out[2:]

        def dense_grads(l, dense, dense_b, one, two, *also):
            one = begin([SIDE_X, SIDE_Y], order(
                lambda *a: in_pair(pos, own_rows, a[:2], a[2:4], a[4:6]),
                saved[l][7], dense, kept[l][2], dense_b, *one, *also,
            ))
            two = begin([SIDE_Y, SIDE_X], order(
                lambda *a: back_pair(pos, own_rows, a[:2], a[2:4], a[4:]),
                dense, saved[l][8], dense_b, kept[l][3], *two,
            ))
            return one, two

        dense, dr1, do, vec = dense_part(1, own, far)
        dense_b = swap(dense)
        joined, own, far_part = attn_part(1, do, dr1, vec, *kept[1])
        far = flip(far_part)
        one, two = attn_grads(1, dense, dense_b, joined, swap(joined))
        x_one, y_one = dense_grads(1, dense, dense_b, one, two, far)
        dense, dr1, do, vec = dense_part(0, own, far)
        dense_b = swap(dense)
        joined, own, far_part = attn_part(0, do, dr1, vec)
        joined_b = swap(joined)
        x_one.turn()
        y_one.turn()
        one, two = attn_grads(0, dense, dense_b, joined, joined_b)
        x_zero, y_zero = dense_grads(0, dense, dense_b, one, two)
        both_one = Together(jnp.stack, x_one, y_one)
        both_one.turn()
    else:
        for l in reversed(range(layers)):
            x_all, _, _, _, _, o, _, h, act, _, _ = saved[l]
            dense, dr1, do, vec = dense_part(l, own, far)
            joined, own, far_part = attn_part(l, do, dr1, vec)
            dk, dv, dq = joined[: 2 * rows], joined[2 * rows : 4 * rows], joined[4 * rows :]
            far = flip(far_part)
            du, df, db = dense[:, :ff], dense[:, ff : ff + width], dense[:, ff + width :]
            grads = [
                jnp.concatenate(
                    [over_rows(x_all[:rows], dq), over_rows(x_all, dk), over_rows(x_all, dv),
                     over_rows(o, db)], axis=1,
                ),
                over_rows(h, du),
                over_rows(act, df).reshape(devices, parts, own_rows, width)
                .transpose(0, 2, 1, 3).reshape(width, ff),
            ]
            shards[l] = [
                lax.psum_scatter(g.astype(BF), AXES, scatter_dimension=0, tiled=True).astype(F4)
                for g in grads
            ]
    sums = order(
        lambda one, two: table_sums(key_columns, own_columns, one, two, line_n, plane_n),
        *score_grads,
    )
    heads = sums.shape[0]
    wide = jnp.concatenate([sums[:, n] for n in range(3)], axis=1)
    wide = jnp.pad(wide, ((0, VEC_GRADS - heads), (0, width - wide.shape[1])))
    flat = jnp.concatenate(vec_grads + [wide], axis=0)
    if split:
        both_one.turn()
        small = Everywhere(devices, order, flat)
        x_zero.turn()
        small.step()
        y_zero.turn()
        small.step()
        both_zero = Together(jnp.stack, x_zero, y_zero)
        both_zero.turn(both_one.came)
        far_part, _ = lax.optimization_barrier((far_part, both_zero.keep))
        far = flip(far_part)
        both_zero.turn(far)
        small.step()
        small.step()
        flat = small.total()
        both_zero.came, both_one.came, flat = lax.optimization_barrier(
            (both_zero.came, both_one.came, flat)
        )
        for l, both in ((0, both_zero), (1, both_one)):
            one, two = both.totals()
            shards[l] = [
                jnp.concatenate([one[:, ff:], two[:, ff:]], axis=1), one[:, :ff], two[:, :ff]
            ]
    else:
        flat = summed_everywhere(flat, devices)
    grad_in = (own + far.astype(F4)).astype(BF)
    sums = flat[layers * VEC_GRADS : layers * VEC_GRADS + heads]
    grad_across = buckets_from_sums(sums[:, :LANES], plane_n)
    grad_upward = buckets_from_sums(sums[:, LANES : 2 * LANES], plane_n)
    grad_line = buckets_from_sums(sums[:, 2 * LANES : 3 * LANES], line_n)

    vec_grad = flat[: layers * VEC_GRADS].reshape(layers, VEC_GRADS, width)
    mine = lax.dynamic_slice_in_dim(vec_grad, me * own_rows, own_rows, axis=2)
    grad_in_bias = lax.dynamic_slice_in_dim(
        vec_grad[:, 3 : 3 + parts].reshape(layers, ff), me * parts * own_rows, parts * own_rows, axis=1
    )
    out_bias_g, gain_one_g, shift_one_g = [mine[:, n] for n in range(3)]
    back_bias_g, gain_two_g, shift_two_g = [mine[:, 3 + parts + n] for n in range(3)]
    query_bias_g, value_bias_g = mine[:, VEC_GRADS - 2], mine[:, VEC_GRADS - 1]

    grad_attn = jnp.stack([shards[l][0] for l in range(layers)])
    grad_inw = jnp.stack([shards[l][1] for l in range(layers)])
    grad_back = jnp.stack(
        [
            jnp.concatenate(
                [shards[l][2][:, g * width : (g + 1) * width] for g in range(parts)], axis=0
            )
            for l in range(layers)
        ]
    )
    return (
        hidden_out, grad_in,
        grad_attn[:, :, : 3 * width], query_bias_g, value_bias_g, grad_attn[:, :, 3 * width :],
        out_bias_g, gain_one_g, shift_one_g,
        grad_inw, grad_in_bias, grad_back, back_bias_g, gain_two_g, shift_two_g,
        grad_line, grad_across, grad_upward,
    )


def solution(mesh):
    devices = mesh.shape["dp"] * mesh.shape["blk"]
    tokens = P(AXES, None)
    weight = P(None, AXES, None)
    vector = P(None, AXES)
    return jax.shard_map(
        functools.partial(on_device, devices),
        mesh=mesh,
        in_specs=(
            tokens, tokens, P("dp"), P(None, AXES),
            weight, vector, vector, weight, vector, vector, vector,
            weight, vector, weight, vector, vector, vector,
            P(), P(), P(),
        ),
        out_specs=(
            tokens, tokens,
            weight, vector, vector, weight, vector, vector, vector,
            weight, vector, weight, vector, vector, vector,
            P(), P(), P(),
        ),
        check_vma=False,
    )
```

```python
import functools
import math

import jax
import jax.numpy as jnp
from jax import lax
from jax.experimental import pallas as pl
from jax.experimental.pallas import tpu as pltpu
from jax.sharding import PartitionSpec as P

REACH_1D = 128
REACH_2D = 256
COORD_TOP = 1000

eps_norm = 1e-12
big_negative = -1e30

BF = jnp.bfloat16
F4 = jnp.float32
AXES = ("dp", "blk")
VMEM = 56 * 1024 * 1024

HEAD = 64
QUAD = 256
LANES = 128


def bucket_marks(bucket_count, far_reach):
    half_count = bucket_count // 2
    exact_limit = half_count // 2
    thresholds = []
    for bucket_step in range(1, half_count):
        if bucket_step < exact_limit:
            thresholds.append(bucket_step)
        else:
            thresholds.append(
                math.ceil(
                    exact_limit
                    * (far_reach / exact_limit)
                    ** ((bucket_step - exact_limit) / (half_count - exact_limit))
                )
            )
    return thresholds


def params(**more):
    return pltpu.CompilerParams(vmem_limit_bytes=VMEM, **more)


def cost(flops, traffic):
    return pl.CostEstimate(
        flops=int(flops / 20), bytes_accessed=int(traffic / 20), transcendentals=0
    )


def mm(left, right):
    return jnp.dot(left, right, preferred_element_type=F4)


def mm_t(left, right):
    return lax.dot_general(left, right, (((1,), (1,)), ((), ())), preferred_element_type=F4)


def over_rows(left, right):
    return lax.dot_general(left, right, (((0,), (0,)), ((), ())), preferred_element_type=F4)


def pick(table_row, codes):
    return jnp.take_along_axis(
        jnp.broadcast_to(table_row, codes.shape), codes, axis=1, mode="promise_in_bounds"
    )


def bias_kernel(heads, line_n, plane_n, scal, own_ref, keys_ref, plane_ref, line_ref, out_ref):
    rows = out_ref.shape[1]
    chunk = 32
    step = pl.program_id(0)
    length, half = scal[0], scal[1]
    magnitude = lax.broadcasted_iota(jnp.int32, (1, LANES), 1)

    def marks(base, count, reach):
        code = jnp.zeros((1, LANES), jnp.int32)
        for mark in bucket_marks(count, reach):
            code = code + (magnitude + base >= mark).astype(jnp.int32)
        return code

    near, far = marks(0, plane_n, REACH_2D), marks(LANES, plane_n, REACH_2D)
    flat = marks(0, line_n, REACH_1D)
    key_index = step * LANES + magnitude
    key_place = jnp.where(
        key_index < rows, half * rows + key_index, (1 - half) * rows + key_index - rows
    )
    live = key_place < length
    across_key, upward_key = keys_ref[0:1, :], keys_ref[1:2, :]

    def plane_code(offset):
        size = jnp.minimum(jnp.abs(offset), 2 * LANES - 1)
        low = jnp.bitwise_and(size, LANES - 1)
        code = jnp.where(size >= LANES, pick(far, low), pick(near, low))
        return code + jnp.where(offset > 0, plane_n // 2, 0)

    def body(index, carry):
        first = pl.multiple_of(index * chunk, chunk)
        span = pl.ds(first, chunk)
        across = plane_code(across_key - own_ref[span, 0:1])
        upward = plane_code(upward_key - own_ref[span, 1:2]) + plane_n
        place = (
            half * rows + first + lax.broadcasted_iota(jnp.int32, (chunk, LANES), 0)
        )
        offset = key_place - place
        along = pick(flat, jnp.minimum(jnp.abs(offset), LANES - 1)) + jnp.where(
            offset > 0, line_n // 2, 0
        )
        for head in range(heads):
            plane_row = plane_ref[head : head + 1, :]
            total = (
                pick(line_ref[head : head + 1, :], along)
                + pick(plane_row, across)
                + pick(plane_row, upward)
            )
            out_ref[head, span, :] = jnp.where(live, total, big_negative)
        return carry

    lax.fori_loop(0, rows // chunk, body, 0)


def score_biases(length, half, own_xy, key_xy, line_table, across_table, upward_table):
    heads = line_table.shape[1]
    rows, keys = own_xy.shape[1], key_xy.shape[1]
    line_n, plane_n = line_table.shape[0], across_table.shape[0]
    plane = jnp.concatenate([across_table, upward_table], axis=0).astype(F4).T
    line = jnp.pad(line_table.astype(F4).T, ((0, 0), (0, LANES - line_n)))
    whole = pl.BlockSpec(memory_space=pltpu.VMEM)
    return pl.pallas_call(
        functools.partial(bias_kernel, heads, line_n, plane_n),
        grid=(keys // LANES,),
        in_specs=[
            pl.BlockSpec(memory_space=pltpu.SMEM),
            whole,
            pl.BlockSpec((2, LANES), lambda j: (0, j)),
            whole,
            whole,
        ],
        out_specs=pl.BlockSpec((heads, rows, LANES), lambda j: (0, 0, j)),
        out_shape=jax.ShapeDtypeStruct((heads, rows, keys), F4),
        compiler_params=params(),
        cost_estimate=cost(3e9, heads * rows * keys * 4),
        name="score_bias",
    )(jnp.stack([length, half]), own_xy.T, key_xy, plane, line)


QUERY_BIAS, VALUE_BIAS, OUT_BIAS, GAIN_ONE, SHIFT_ONE, BACK_BIAS, GAIN_TWO, SHIFT_TWO = range(8)
VECS = 8
VEC_GRADS = 16


def pack_kernel(own_rows, qkv, out, inw, back, first, second, packed):
    layers, _, width = out.shape
    ff = inw.shape[2]
    base = 0
    for l in range(layers):
        if l == 0:
            first[...] = qkv[l, :, : 2 * width]
            second[:, :width] = qkv[l, :, 2 * width :]
            second[:, width:] = out[l]
        else:
            packed[:, base : base + 3 * width] = qkv[l]
            packed[:, base + 3 * width : base + 4 * width] = out[l]
            base += 4 * width
        packed[:, base : base + ff] = inw[l]
        base += ff
        wide = back[l].astype(F4)
        for g in range(ff // width):
            packed[:, base : base + width] = wide[g * own_rows : (g + 1) * own_rows].astype(BF)
            base += width


def pack(qkv, out, inw, back):
    layers, own_rows, width = out.shape
    ff = inw.shape[2]
    columns = (layers - 1) * 4 * width + layers * 2 * ff
    shape = lambda n: jax.ShapeDtypeStruct((own_rows, n), BF)
    return pl.pallas_call(
        functools.partial(pack_kernel, own_rows),
        out_shape=[shape(2 * width), shape(2 * width), shape(columns)],
        compiler_params=params(),
        name="pack_weights",
    )(qkv, out, inw, back)


class Weights:
    def __init__(self, layer, first, second, packed, parts):
        if layer == 0:
            self.q, self.k, self.v, self.o = (first, 0), (first, 1), (second, 0), (second, 1)
            base = 0
        else:
            base = 2 * parts + (layer - 1) * (4 + 2 * parts)
            self.q, self.k, self.v, self.o = [(packed, base + n) for n in range(4)]
            base += 4
        self.inw, self.back = (packed, base), (packed, base + parts)


def head_masks(dtype):
    lane = lax.broadcasted_iota(jnp.int32, (1, QUAD), 1)
    return [
        ((lane >= h * HEAD) & (lane < (h + 1) * HEAD)).astype(dtype) for h in range(QUAD // HEAD)
    ]


def attn_fwd_kernel(x_ref, wq, wk, wv, vec, bias_ref, q_out, k_out, v_out, p_out, o_out):
    rows = q_out.shape[0]
    x = x_ref[...]
    q = ((mm(x[:rows], wq[...]) + vec[QUERY_BIAS : QUERY_BIAS + 1]) * 0.125).astype(BF)
    k = mm(x, wk[...]).astype(BF)
    v = (mm(x, wv[...]) + vec[VALUE_BIAS : VALUE_BIAS + 1]).astype(BF)
    q_out[...] = q
    k_out[...] = k
    v_out[...] = v
    lane = lax.broadcasted_iota(jnp.int32, (rows, QUAD), 1)
    mixed = jnp.zeros((rows, QUAD), F4)
    for h, mask in enumerate(head_masks(BF)):
        s = mm_t(q * mask, k) + bias_ref[h]
        e = jnp.exp(s - jnp.max(s, axis=-1, keepdims=True))
        p = (e * (1.0 / jnp.sum(e, axis=-1, keepdims=True))).astype(BF)
        p_out[h] = p
        mixed = jnp.where((lane >= h * HEAD) & (lane < (h + 1) * HEAD), mm(p, v), mixed)
    o_out[...] = mixed.astype(BF)


def attn_fwd(layer, x_all, weights, vecs, bias):
    keys, width = x_all.shape
    heads, rows, _ = bias.shape
    quads = width // QUAD
    per = QUAD // HEAD
    weight = lambda place: pl.BlockSpec((width, QUAD), lambda j: (0, place[1] * quads + j))
    cols = lambda n: pl.BlockSpec((n, QUAD), lambda j: (0, j))
    scores = pl.BlockSpec((per, rows, keys), lambda j: (j, 0, 0))
    sds = jax.ShapeDtypeStruct
    return pl.pallas_call(
        attn_fwd_kernel,
        grid=(quads,),
        in_specs=[
            pl.BlockSpec((keys, width), lambda j: (0, 0)),
            weight(weights.q),
            weight(weights.k),
            weight(weights.v),
            pl.BlockSpec((VECS, QUAD), lambda j: (layer, j)),
            scores,
        ],
        out_specs=[cols(rows), cols(keys), cols(keys), scores, cols(rows)],
        out_shape=[
            sds((rows, width), BF),
            sds((keys, width), BF),
            sds((keys, width), BF),
            sds((heads, rows, keys), BF),
            sds((rows, width), BF),
        ],
        compiler_params=params(),
        cost_estimate=cost(8e9, 16e6),
        name="attention_forward",
    )(x_all, weights.q[0], weights.k[0], weights.v[0], vecs, bias)


def normed(values):
    centered = values - jnp.mean(values, axis=-1, keepdims=True)
    variance = jnp.mean(centered * centered, axis=-1, keepdims=True)
    scale = lax.rsqrt(variance + eps_norm)
    return centered * scale, scale


def natural_rows(own_rows, block, width):
    parts = block.shape[1] // width
    devices = block.shape[0] // own_rows
    wide = [
        block[:, g * width : (g + 1) * width].astype(F4).reshape(devices, 1, own_rows, width)
        for g in range(parts)
    ]
    return jnp.concatenate(wide, axis=1).reshape(devices * parts * own_rows, width).astype(BF)


def ffn_fwd_kernel(
    own_rows, x_ref, o_ref, wo, win, wback, vec, bin_,
    r1_out, h_out, act_out, slope_out, r2_out, x_out, low_out, middle, total,
):
    step = pl.program_id(0)
    width = x_ref.shape[1]
    row = lambda k: vec[k : k + 1]

    @pl.when(step == 0)
    def _():
        r1 = x_ref[...].astype(F4) + mm(o_ref[...], wo[...]) + row(OUT_BIAS)
        r1_out[...] = r1
        n, _ = normed(r1)
        h = n * row(GAIN_ONE) + row(SHIFT_ONE)
        middle[...] = h
        h_out[...] = h.astype(BF)
        total[...] = jnp.zeros_like(total)

    u = mm(h_out[...], win[...]) + bin_[...]
    cdf = 0.5 * (1.0 + lax.erf(u * 0.7071067811865476))
    act = (u * cdf).astype(BF)
    act_out[...] = act
    slope_out[...] = (cdf + u * (0.3989422804014327 * jnp.exp(-0.5 * u * u))).astype(BF)
    total[...] += mm(act, natural_rows(own_rows, wback[...], width))

    @pl.when(step == pl.num_programs(0) - 1)
    def _():
        r2 = middle[...] + total[...] + row(BACK_BIAS)
        r2_out[...] = r2
        n, _ = normed(r2)
        x = n * row(GAIN_TWO) + row(SHIFT_TWO)
        x_out[...] = x
        low_out[...] = x.astype(BF)


def ffn_fwd(layer, x, o, weights, vecs, in_biases, own_rows):
    rows, width = x.shape
    ff = in_biases.shape[1]
    parts = ff // width
    full = pl.BlockSpec((rows, width), lambda j: (0, 0))
    chunk = pl.BlockSpec((rows, width), lambda j: (0, j))
    sds = jax.ShapeDtypeStruct
    return pl.pallas_call(
        functools.partial(ffn_fwd_kernel, own_rows),
        grid=(parts,),
        in_specs=[
            full,
            full,
            pl.BlockSpec((width, width), lambda j: (0, weights.o[1])),
            pl.BlockSpec((width, width), lambda j: (0, weights.inw[1] + j)),
            pl.BlockSpec((width // parts, ff), lambda j: (j, weights.back[1] // parts)),
            pl.BlockSpec((VECS, width), lambda j: (layer, 0)),
            pl.BlockSpec((1, width), lambda j: (0, layer * parts + j)),
        ],
        out_specs=[full, full, chunk, chunk, full, full, full],
        out_shape=[
            sds((rows, width), F4),
            sds((rows, width), BF),
            sds((rows, ff), BF),
            sds((rows, ff), BF),
            sds((rows, width), F4),
            sds((rows, width), F4),
            sds((rows, width), BF),
        ],
        scratch_shapes=[pltpu.VMEM((rows, width), F4), pltpu.VMEM((rows, width), F4)],
        compiler_params=params(),
        cost_estimate=cost(9e9, 20e6),
        name="dense_forward",
    )(x, o, weights.o[0], weights.inw[0], weights.back[0], vecs, in_biases.reshape(1, -1))


def norm_back(grad, values, gain):
    n, scale = normed(values)
    e = grad * gain
    inner = jnp.mean(e * n, axis=-1, keepdims=True)
    out = (e - jnp.mean(e, axis=-1, keepdims=True) - n * inner) * scale
    return out, jnp.sum(grad * n, axis=0, keepdims=True), jnp.sum(grad, axis=0, keepdims=True)


def ffn_bwd_kernel(
    own_rows, own_ref, far_ref, r2_ref, vec, wback, slope, win, r1_ref, wo,
    joined, dr1_out, do_out, vec_out, dr2, total,
):
    step = pl.program_id(0)
    width = own_ref.shape[1]
    end = pl.num_programs(0) - 1
    ff = joined.shape[1] - 2 * width

    @pl.when(step == 0)
    def _():
        grad = own_ref[...] + far_ref[...].astype(F4)
        out, gain, shift = norm_back(grad, r2_ref[...], vec[GAIN_TWO : GAIN_TWO + 1])
        dr2[...] = out
        low = out.astype(BF)
        joined[:, ff : ff + width] = low
        vec_out[...] = jnp.zeros_like(vec_out)
        vec_out[3 + end + 1 : 3 + end + 2, :] = jnp.sum(low.astype(F4), axis=0, keepdims=True)
        vec_out[3 + end + 2 : 3 + end + 3, :] = gain
        vec_out[3 + end + 3 : 3 + end + 4, :] = shift
        total[...] = jnp.zeros_like(total)

    back = natural_rows(own_rows, wback[...], width)
    du = (mm_t(joined[:, ff : ff + width], back) * slope[...].astype(F4)).astype(BF)

    vec_out[pl.ds(3 + step, 1), :] = jnp.sum(du.astype(F4), axis=0, keepdims=True)

    joined[:, pl.ds(pl.multiple_of(step * width, width), width)] = du
    total[...] += mm_t(du, win[...])

    @pl.when(step == pl.num_programs(0) - 1)
    def _():
        out, gain, shift = norm_back(
            dr2[...] + total[...], r1_ref[...], vec[GAIN_ONE : GAIN_ONE + 1]
        )
        dr1_out[...] = out
        low = out.astype(BF)
        joined[:, ff + width :] = low
        vec_out[0:1, :] = jnp.sum(low.astype(F4), axis=0, keepdims=True)
        vec_out[1:2, :] = gain
        vec_out[2:3, :] = shift
        do_out[...] = mm_t(low, wo[...]).astype(BF)


def ffn_bwd(layer, own, far, r2, vecs, slope, weights, r1, own_rows):
    rows, width = own.shape
    ff = slope.shape[1]
    parts = ff // width
    full = pl.BlockSpec((rows, width), lambda j: (0, 0))
    chunk = pl.BlockSpec((rows, width), lambda j: (0, j))
    sds = jax.ShapeDtypeStruct
    return pl.pallas_call(
        functools.partial(ffn_bwd_kernel, own_rows),
        grid=(parts,),
        in_specs=[
            full, full, full,
            pl.BlockSpec((VECS, width), lambda j: (layer, 0)),
            pl.BlockSpec((width // parts, ff), lambda j: (j, weights.back[1] // parts)),
            chunk,
            pl.BlockSpec((width, width), lambda j: (0, weights.inw[1] + j)),
            full,
            pl.BlockSpec((width, width), lambda j: (0, weights.o[1])),
        ],
        out_specs=[
            pl.BlockSpec((rows, ff + 2 * width), lambda j: (0, 0)),
            full, full,
            pl.BlockSpec((VEC_GRADS, width), lambda j: (0, 0)),
        ],
        out_shape=[
            sds((rows, ff + 2 * width), BF),
            sds((rows, width), F4),
            sds((rows, width), BF),
            sds((VEC_GRADS, width), F4),
        ],
        scratch_shapes=[pltpu.VMEM((rows, width), F4), pltpu.VMEM((rows, width), F4)],
        compiler_params=params(),
        cost_estimate=cost(9e9, 20e6),
        name="dense_backward",
    )(own, far, r2, vecs, weights.back[0], slope, weights.inw[0], r1, weights.o[0])


def attn_bwd_kernel(
    q_ref, k_ref, v_ref, p_ref, do_ref, wq, wk, wv, dr1_ref, vec_ref,
    joined, ds_out, own_out, far_out, vec_out, far_sum,
):
    step = pl.program_id(0)
    rows = q_ref.shape[0]

    @pl.when(step == 0)
    def _():
        own_out[...] = dr1_ref[...]
        far_sum[...] = jnp.zeros_like(far_sum)

    q, k, v, do = q_ref[...], k_ref[...], v_ref[...], do_ref[...]
    q_t, do_t = q.T, do.T
    lane = lax.broadcasted_iota(jnp.int32, (rows, QUAD), 1)
    dq = jnp.zeros((rows, QUAD), F4)
    dk_t, dv_t = [], []
    for h, mask in enumerate(head_masks(BF)):
        low = p_ref[h]
        p = low.astype(F4)
        t = p * mm_t(do * mask, v)
        ds = (t - p * jnp.sum(t, axis=-1, keepdims=True)).astype(BF)
        ds_out[h] = ds
        dq = jnp.where((lane >= h * HEAD) & (lane < (h + 1) * HEAD), mm(ds, k), dq)
        dk_t.append(mm(q_t[h * HEAD : (h + 1) * HEAD], ds))
        dv_t.append(mm(do_t[h * HEAD : (h + 1) * HEAD], low))
    dk = jnp.concatenate(dk_t, axis=0).T.astype(BF)
    dv = jnp.concatenate(dv_t, axis=0).T.astype(BF)
    dq = (dq.astype(BF).astype(F4) * 0.125).astype(BF)
    keys = k.shape[0]
    joined[:keys] = dk
    joined[keys : 2 * keys] = dv
    joined[2 * keys :] = dq
    vec_out[: VEC_GRADS - 2] = vec_ref[: VEC_GRADS - 2]
    vec_out[VEC_GRADS - 2 : VEC_GRADS - 1] = jnp.sum(dq.astype(F4), axis=0, keepdims=True)
    vec_out[VEC_GRADS - 1 :] = jnp.sum(dv.astype(F4), axis=0, keepdims=True)
    both = mm_t(dk, wk[...]) + mm_t(dv, wv[...])
    own_out[...] += mm_t(dq, wq[...]) + both[:rows]
    far_sum[...] += both[rows:]

    @pl.when(step == pl.num_programs(0) - 1)
    def _():
        far_out[...] = far_sum[...].astype(BF)


def attn_bwd(q, k, v, p, do, weights, dr1, vec):
    heads, rows, keys = p.shape
    width = q.shape[1]
    quads = width // QUAD
    per = QUAD // HEAD
    weight = lambda place: pl.BlockSpec((width, QUAD), lambda j: (0, place[1] * quads + j))
    cols = lambda n: pl.BlockSpec((n, QUAD), lambda j: (0, j))
    scores = pl.BlockSpec((per, rows, keys), lambda j: (j, 0, 0))
    full = pl.BlockSpec((rows, width), lambda j: (0, 0))
    sds = jax.ShapeDtypeStruct
    return pl.pallas_call(
        attn_bwd_kernel,
        grid=(quads,),
        in_specs=[
            cols(rows), cols(keys), cols(keys), scores, cols(rows),
            weight(weights.q), weight(weights.k), weight(weights.v), full,
            cols(VEC_GRADS),
        ],
        out_specs=[
            cols(2 * keys + rows), scores, full, full,
            cols(VEC_GRADS),
        ],
        out_shape=[
            sds((2 * keys + rows, width), BF),
            sds((heads, rows, keys), BF),
            sds((rows, width), F4),
            sds((rows, width), BF),
            sds((VEC_GRADS, width), F4),
        ],
        scratch_shapes=[pltpu.VMEM((rows, width), F4)],
        compiler_params=params(),
        cost_estimate=cost(10e9, 20e6),
        name="attention_backward",
    )(q, k, v, p, do, weights.q[0], weights.k[0], weights.v[0], dr1, vec)


CORE, SIDE_X, SIDE_Y, TOP = 2, 1, 4, 8
EVERY = slice(None)


def core_rows(pos, block, group_rows):
    block = block.reshape(block.shape[0] // (2 * group_rows), 2, group_rows, block.shape[1])
    return jnp.where(pos[0] == 0, block[:, 0], block[:, 1]).reshape(-1, block.shape[3])


def part_along(first, grad, own_rows):
    inner = own_rows if first == SIDE_X else 2 * own_rows
    grad = grad.reshape(grad.shape[0] // (2 * inner), 2, inner, grad.shape[1])
    return grad[:, 0].reshape(-1, grad.shape[3]), grad[:, 1].reshape(-1, grad.shape[3])


def put(first, pos, zero, one, outs, where=(EVERY, EVERY)):
    low = pos[1 if first == SIDE_X else 2] == 0
    outs[0][where] = jnp.where(low, zero, one).astype(BF)
    outs[1][where] = jnp.where(low, one, zero).astype(BF)


def attn_pair_kernel(own_rows, pos, x_a, g_a, o_a, e_a, x_b, g_b, o_b, e_b, _, __, ___, ____,
                     keep, send, keep_too, send_too, t_a, t_b):
    step = pl.program_id(0)
    rows, keys = o_a.shape[0], x_a.shape[0]

    def emit(grad, first=SIDE_X, outs=(keep, send)):
        put(first, pos, *part_along(first, grad, own_rows), outs)

    @pl.when(step == 0)
    def _():
        t_a[...] = core_rows(pos, x_a[...].T, 2 * own_rows)
        t_b[...] = core_rows(pos, x_b[...].T, 2 * own_rows)
        emit(mm(t_a[:, :rows], g_a[2 * keys :]) + mm(t_b[:, :rows], g_b[2 * keys :]))

    @pl.when(step == 1)
    def _():
        emit(mm(t_a[...], g_a[:keys]) + mm(t_b[...], g_b[:keys]))

    @pl.when(step == 2)
    def _():
        emit(mm(t_a[...], g_a[keys : 2 * keys]) + mm(t_b[...], g_b[keys : 2 * keys]), SIDE_Y, (keep_too, send_too))

    @pl.when(step == 3)
    def _():
        left = core_rows(pos, o_a[...].T, 2 * own_rows)
        right = core_rows(pos, o_b[...].T, 2 * own_rows)
        emit(mm(left, e_a[...]) + mm(right, e_b[...]), SIDE_Y, (keep_too, send_too))


def in_pair_kernel(own_rows, pos, h_a, u_a, h_b, u_b, keep, send, t_a, t_b):
    @pl.when(pl.program_id(0) == 0)
    def _():
        t_a[...] = core_rows(pos, h_a[...].T, 2 * own_rows)
        t_b[...] = core_rows(pos, h_b[...].T, 2 * own_rows)

    grad = mm(t_a[...], u_a[...]) + mm(t_b[...], u_b[...])
    put(SIDE_X, pos, *part_along(SIDE_X, grad, own_rows), (keep, send))


def back_pair_kernel(own_rows, pos, f_a, a_a, f_b, a_b, keep, send):
    width = f_a.shape[1]
    parts = a_a.shape[1] // (TOP * own_rows)
    inner = 2 * parts * own_rows
    grad = mm(core_rows(pos, a_a[...].T, inner), f_a[...]) + mm(
        core_rows(pos, a_b[...].T, inner), f_b[...]
    )
    grad = grad.reshape(2, 2, parts, own_rows, width)
    for g in range(parts):
        zero = grad[0, :, g].reshape(2 * own_rows, width)
        one = grad[1, :, g].reshape(2 * own_rows, width)
        put(SIDE_Y, pos, zero, one, (keep, send), (EVERY, slice(g * width, (g + 1) * width)))


def attn_pair(pos, own_rows, mine, theirs, groups):
    keys, width = mine[0].shape
    rows, last = mine[3].shape
    base = groups[0].shape[1] // width - 2
    whole = lambda block: pl.BlockSpec(block.shape, lambda j: (0, 0))
    turned = pltpu.VMEM((width // 2, keys), BF)
    specs = [whole(block) for block in mine[:3]]
    specs.append(pl.BlockSpec((rows, width), lambda j: (0, last // width - 1)))
    early = pl.BlockSpec((width // 4, width), lambda j: (0, base + jnp.minimum(j, 1)))
    late = pl.BlockSpec((width // 4, width), lambda j: (0, base + jnp.maximum(j - 2, 0)))
    return pl.pallas_call(
        functools.partial(attn_pair_kernel, own_rows),
        grid=(4,),
        in_specs=[pl.BlockSpec(memory_space=pltpu.SMEM)] + specs * 2
        + [pl.BlockSpec(memory_space=pl.ANY)] * 4,
        out_specs=[early, early, late, late],
        out_shape=[jax.ShapeDtypeStruct(block.shape, BF) for block in groups],
        input_output_aliases={9 + n: n for n in range(4)},
        scratch_shapes=[turned, turned],
        compiler_params=params(),
        cost_estimate=cost(4e9, 8e6),
        name="attention_weight_gradients",
    )(pos, *mine, *theirs, *groups)


def pair_call(body, pos, arrays, specs, grid, shape, out_spec, scratch, name):
    return pl.pallas_call(
        body,
        grid=grid,
        in_specs=[pl.BlockSpec(memory_space=pltpu.SMEM)] + specs,
        out_specs=[out_spec] * 2,
        out_shape=[jax.ShapeDtypeStruct(shape, BF)] * 2,
        scratch_shapes=scratch,
        compiler_params=params(),
        cost_estimate=cost(4e9, 8e6),
        name=name,
    )(pos, *arrays)


def in_pair(pos, own_rows, mine, theirs):
    rows, width = mine[0].shape
    full = pl.BlockSpec((rows, width), lambda j: (0, 0))
    chunk = pl.BlockSpec((rows, width), lambda j: (0, j))
    turned = pltpu.VMEM((width // 2, rows), BF)
    return pair_call(
        functools.partial(in_pair_kernel, own_rows), pos, [*mine, *theirs],
        [full, chunk] * 2, (mine[1].shape[1] // width - 2,), (width // 4, mine[1].shape[1]),
        pl.BlockSpec((width // 4, width), lambda j: (0, j)), [turned, turned],
        "in_weight_gradients",
    )


def back_pair(pos, own_rows, mine, theirs):
    rows, ff = mine[1].shape
    width = (mine[0].shape[1] - ff) // 2
    full = pl.BlockSpec((rows, width), lambda j: (0, ff // width))
    tops = width // (TOP * own_rows)
    chunk = pl.BlockSpec((rows, ff // tops), lambda j: (0, j))
    return pair_call(
        functools.partial(back_pair_kernel, own_rows), pos, [*mine, *theirs],
        [full, chunk] * 2, (tops,), (width // 4, ff + 2 * width),
        pl.BlockSpec((width // (4 * tops), ff), lambda j: (j, 0)), [],
        "back_weight_gradients",
    )


def cut(total, index, inner):
    total = total.reshape(total.shape[0] // (2 * inner), 2, inner, total.shape[1])
    pick_one = lambda i: lax.dynamic_index_in_dim(total, i, 1, keepdims=False)
    return [pick_one(i).reshape(-1, total.shape[3]) for i in (index, 1 - index)]


def fold(keep, came, index, inner):
    k, s = cut(keep, index, inner), cut(came, index, inner)
    return [(a.astype(F4) + b.astype(F4)).astype(BF) for a, b in zip(k, s)]


class Sum:
    def __init__(self, devices, me, own_rows, order, axes, pair):
        tops, top = [], TOP
        while top < devices:
            tops.append(top)
            top *= 2
        self.axes = list(axes) + tops
        self.devices, self.me, self.own_rows, self.order = devices, me, own_rows, order
        self.send(*pair)

    def send(self, keep, send):
        self.keep = keep
        self.came = exchange(send, self.devices, self.axes.pop(0))

    def turn(self):
        axis = self.axes[0]
        inner = self.own_rows * (2 if axis == SIDE_Y and SIDE_X in self.axes else 1)
        index = jnp.bitwise_and(self.me // axis, 1)
        self.send(*self.order(lambda k, c: fold(k, c, index, inner), self.keep, self.came))

    def total(self):
        return self.keep.astype(F4) + self.came.astype(F4)


class Together:
    def __init__(self, joined, *groups):
        self.joined, self.groups = joined, groups
        self.axes, self.devices, self.me = groups[0].axes, groups[0].devices, groups[0].me
        self.own_rows, self.order = groups[0].own_rows, groups[0].order
        self.keep = None

    def turn(self, *also):
        axis = self.axes.pop(0)
        index = jnp.bitwise_and(self.me // axis, 1)

        def halved(keep, came):
            total = keep.astype(F4) + came.astype(F4)
            count, rows, columns = total.shape
            total = total.reshape(count, rows // (2 * self.own_rows), 2, self.own_rows, columns)
            one = lambda i: lax.dynamic_index_in_dim(total, i, 2, keepdims=False)
            shape = (count, rows // 2, columns)
            return [one(i).reshape(shape).astype(BF) for i in (index, 1 - index)]

        if self.keep is None:
            keep, send = self.order(
                lambda keeps, cames, *_: halved(self.joined(keeps), self.joined(cames)),
                [g.keep for g in self.groups], [g.came for g in self.groups], *also,
            )
        else:
            keep, send = self.order(lambda k, c, *_: halved(k, c), self.keep, self.came, *also)
        self.keep, self.came = keep, exchange(send, self.devices, axis)

    def totals(self):
        return list(self.keep.astype(F4) + self.came.astype(F4))


class Everywhere:
    def __init__(self, devices, order, block):
        tops, top = [], TOP
        while top < devices:
            tops.append(top)
            top *= 2
        self.axes = [CORE] + tops + [SIDE_X, SIDE_Y]
        self.devices, self.order = devices, order
        self.send(block)

    def send(self, block):
        self.block, self.came = block, exchange(block, self.devices, self.axes.pop(0))

    def step(self):
        self.send(self.order(lambda b, c: b + c, self.block, self.came))

    def total(self):
        return self.block + self.came


class Order:
    def __init__(self):
        self.last = None

    def __call__(self, call, *arrays):
        if self.last is not None:
            arrays, _ = lax.optimization_barrier((arrays, self.last))
        out = call(*arrays)
        self.last = jax.tree.leaves(out)[0]
        return out


def edge_row(count, reach):
    half = count // 2
    marks = bucket_marks(count, reach)
    lane = lax.broadcasted_iota(jnp.int32, (1, LANES), 1)
    edges = jnp.full((1, LANES), -(1 << 20), jnp.int32)
    for k, mark in enumerate(marks):
        edges = jnp.where(lane == k, 1 - mark, edges)
        edges = jnp.where(lane == half - 1 + k, mark, edges)
    return jnp.where(lane == 2 * half - 2, 1 << 20, edges)


def tables_kernel(
    line_n, plane_n, keys_ref, own_ref, one_ref, two_ref, out_ref, steps, line_steps, spots
):
    keys, rows = keys_ref.shape[0], own_ref.shape[0]
    span = steps.shape[2]

    @pl.when(pl.program_id(0) == 0)
    def _():
        place = lax.broadcasted_iota(jnp.int32, (keys, span), 1)
        for plane in range(2):
            steps[plane] = (keys_ref[:, plane : plane + 1] < place).astype(F4).astype(BF)
            spots[plane] = jnp.clip(
                own_ref[:, plane : plane + 1] + edge_row(plane_n, REACH_2D), 0, COORD_TOP + 1
            )
        line_place = lax.broadcasted_iota(jnp.int32, (keys, keys), 1)
        line_steps[...] = (keys_ref[:, 2:3] <= line_place).astype(F4).astype(BF)
        spots[2] = jnp.clip(own_ref[:, 2:3] + edge_row(line_n, REACH_1D), 0, keys) - 1

    one, two = one_ref[0], two_ref[0]

    def collect(sums, spot):
        safe = jnp.maximum(spot, 0)
        low = jnp.bitwise_and(safe, LANES - 1)
        block = lax.shift_right_logical(safe, 7)
        found = jnp.zeros(spot.shape, F4)
        for b in range(sums.shape[1] // LANES):
            piece = jnp.take_along_axis(
                sums[:, b * LANES : (b + 1) * LANES], low, axis=1, mode="promise_in_bounds"
            )
            found = jnp.where(block == b, piece, found)
        return jnp.sum(jnp.where(spot >= 0, found, 0.0), axis=0, keepdims=True)

    for plane in range(2):
        sums = mm(one, steps[plane]) + mm(two, steps[plane])
        out_ref[0, plane : plane + 1, :] = collect(sums, spots[plane])
    sums = mm(one, line_steps[...]) + mm(two, line_steps[...])
    out_ref[0, 2:3, :] = collect(sums, spots[2])


def table_sums(key_columns, own_columns, one, two, line_n, plane_n):
    heads, rows, keys = one.shape
    span = -(-(COORD_TOP + 2) // LANES) * LANES
    whole = pl.BlockSpec(memory_space=pltpu.VMEM)
    scores = pl.BlockSpec((1, rows, keys), lambda j: (j, 0, 0))
    return pl.pallas_call(
        functools.partial(tables_kernel, line_n, plane_n),
        grid=(heads,),
        in_specs=[whole, whole, scores, scores],
        out_specs=pl.BlockSpec((1, 8, LANES), lambda j: (j, 0, 0)),
        out_shape=jax.ShapeDtypeStruct((heads, 8, LANES), F4),
        scratch_shapes=[
            pltpu.VMEM((2, keys, span), BF),
            pltpu.VMEM((keys, keys), BF),
            pltpu.VMEM((3, rows, LANES), jnp.int32),
        ],
        compiler_params=params(),
        cost_estimate=cost(16e9, 6e6),
        name="table_sums",
    )(key_columns, own_columns, one, two)


def buckets_from_sums(sums, count):
    half = count // 2
    below, above = sums[:, : half - 1], sums[:, half - 1 : 2 * half - 2]
    total = sums[:, 2 * half - 2 : 2 * half - 1]
    zero = jnp.zeros_like(total)
    lower = jnp.concatenate([above[:, :1], below], axis=1) - jnp.concatenate([below, zero], axis=1)
    upper = jnp.concatenate([above[:, 1:], total], axis=1) - above
    return jnp.concatenate([lower, zero, upper], axis=1).T


def exchange(block, devices, distance):
    return lax.ppermute(block, AXES, [(i, i ^ distance) for i in range(devices)])


def summed_everywhere(block, devices):
    distance = 1
    while distance < devices:
        block = block + exchange(block, devices, distance)
        distance *= 2
    return block


def all_rows(block, devices, me, axes):
    rows, columns = block.shape
    block = block[None]
    had = []
    for axis in axes:
        came = exchange(block, devices, axis)
        upper = jnp.bitwise_and(me // axis, 1) == 1
        inner = 1
        for other in had:
            inner *= 2 if other < axis else 1
        shape = (block.shape[0] // inner, 1, inner, rows, columns)
        mine, theirs = block.reshape(shape), came.reshape(shape)
        block = jnp.where(
            upper,
            jnp.concatenate([theirs, mine], axis=1),
            jnp.concatenate([mine, theirs], axis=1),
        ).reshape(-1, rows, columns)
        had.append(axis)
    return block.reshape(-1, columns)


def gathered_small(block, devices, me):
    count = 1
    block = block[None]
    while count < devices:
        came = exchange(block, devices, count)
        upper = jnp.bitwise_and(me // count, 1) == 1
        block = jnp.concatenate(
            [jnp.where(upper, came, block), jnp.where(upper, block, came)], axis=0
        )
        count *= 2
    return block


def on_device(
    devices,
    hidden_in, cotangent, lengths, coords,
    qkv_weight, query_bias, value_bias, out_weight, out_bias, norm1_gain, norm1_shift,
    in_weight, in_bias, back_weight, back_bias, norm2_gain, norm2_shift,
    line_table, horizontal_table, vertical_table,
):
    rows, width = hidden_in.shape
    layers, own_rows, _ = qkv_weight.shape
    ff = in_weight.shape[2]
    parts = ff // width
    line_n, plane_n = line_table.shape[0], horizontal_table.shape[0]
    half = lax.axis_index("blk")
    me = lax.axis_index(AXES)
    length = lengths[0]
    flip = lambda block: exchange(block, devices, 1)
    split = own_rows % 8 == 0

    first, second, packed = pack(qkv_weight, out_weight, in_weight, back_weight)
    packed = lax.all_gather(packed, AXES, axis=0, tiled=True)
    if split:
        tops = [top for top in (TOP << n for n in range(devices)) if top < devices][::-1]
        first = all_rows(first, devices, me, tops + [SIDE_Y, SIDE_X, CORE])
        second = all_rows(second, devices, me, tops + [SIDE_X, SIDE_Y, CORE])
    else:
        first = lax.all_gather(first, AXES, axis=0, tiled=True)
        second = lax.all_gather(second, AXES, axis=0, tiled=True)
    far_x = flip(hidden_in)
    far_coords = flip(coords)
    vec_local = jnp.stack(
        [query_bias, value_bias, out_bias, norm1_gain, norm1_shift, back_bias, norm2_gain,
         norm2_shift], axis=1,
    ).reshape(layers * VECS, own_rows)
    in_local = in_bias.reshape(layers * parts, own_rows)
    small = gathered_small(
        jnp.concatenate([vec_local, in_local], axis=0).astype(F4), devices, me
    )
    vecs = small[:, : layers * VECS].transpose(1, 0, 2).reshape(layers * VECS, width)
    in_biases = (
        small[:, layers * VECS :]
        .reshape(devices, layers, parts * own_rows)
        .transpose(1, 0, 2)
        .reshape(layers, ff)
    )
    key_coords = jnp.concatenate([coords, far_coords], axis=1)
    bias = score_biases(
        length, half, coords, key_coords, line_table, horizontal_table, vertical_table
    )

    weights = [Weights(l, first, second, packed, parts) for l in range(layers)]
    state, low = hidden_in, hidden_in
    saved, kept = [], []
    for l in range(layers):
        if l > 0:
            far_x = flip(low)
        if kept:
            far_x, *kept[-1] = lax.optimization_barrier((far_x, *kept[-1]))
        x_all = jnp.concatenate([low, far_x], axis=0)
        q, k, v, p, o = attn_fwd(l, x_all, weights[l], vecs, bias)
        r1, h, act, slope, r2, state, low = ffn_fwd(
            l, state, o, weights[l], vecs, in_biases, own_rows
        )
        saved.append((x_all, q, k, v, p, o, r1, h, act, slope, r2))
        if split:
            kept.append([exchange(block, devices, CORE) for block in (x_all, o, h, act)])
    hidden_out = low

    place = half * rows + jnp.arange(rows, dtype=jnp.int32)
    other = (1 - half) * rows + jnp.arange(rows, dtype=jnp.int32)
    key_columns = jnp.concatenate(
        [key_coords, jnp.concatenate([place, other])[None]], axis=0
    ).T
    own_columns = jnp.concatenate([coords, place[None]], axis=0).T
    own = jnp.where((place < length)[:, None], cotangent.astype(F4), 0.0)
    far = jnp.zeros((rows, width), BF)
    bit = lambda mask: jnp.bitwise_and(me // mask, 1).astype(jnp.int32)
    pos = jnp.stack([bit(CORE), bit(SIDE_X), bit(SIDE_Y)])
    top = (me // TOP).astype(jnp.int32)
    vec_grads = [None] * layers
    score_grads = [None] * layers
    order = Order()
    swap = lambda block: exchange(block, devices, CORE)
    begin = lambda axes, pair: Sum(devices, me, own_rows, order, axes, pair)

    def dense_part(l, own, far, *also):
        r2, r1, slope = saved[l][10], saved[l][6], saved[l][9]
        return order(
            lambda own, far, *_: ffn_bwd(l, own, far, r2, vecs, slope, weights[l], r1, own_rows),
            own, far, *also,
        )

    def attn_part(l, do, dr1, vec, *also):
        q, k, v, p = saved[l][1:5]
        out = order(
            lambda do, dr1, vec, *_: attn_bwd(q, k, v, p, do, weights[l], dr1, vec),
            do, dr1, vec, *also,
        )
        *out, score_grads[l], own, far_part, vec_grads[l] = out
        return *out, own, far_part

    shards = [None] * layers
    if split:

        def weight_grads(l, dense, dense_b, joined, joined_b, *also):
            x_b, o_b, h_b, act_b = kept[l]
            one = order(
                lambda *a: in_pair(pos, own_rows, a[:2], a[2:]), saved[l][7], dense, h_b, dense_b
            )
            two = order(
                lambda *a: back_pair(pos, own_rows, a[:2], a[2:]), dense, saved[l][8], dense_b, act_b
            )
            out = order(
                lambda *a: attn_pair(pos, own_rows, a[:4], a[4:8], a[8:12]),
                saved[l][0], joined, saved[l][5], dense, x_b, joined_b, o_b, dense_b, *one, *two, *also,
            )
            return begin([SIDE_X, SIDE_Y], out[:2]), begin([SIDE_Y, SIDE_X], out[2:])

        dense, dr1, do, vec = dense_part(1, own, far)
        dense_b = swap(dense)
        joined, own, far_part = attn_part(1, do, dr1, vec, *kept[1])
        far = flip(far_part)
        x_one, y_one = weight_grads(1, dense, dense_b, joined, swap(joined), far)
        dense, dr1, do, vec = dense_part(0, own, far)
        dense_b = swap(dense)
        joined, own, far_part = attn_part(0, do, dr1, vec)
        joined_b = swap(joined)
        x_one.turn()
        y_one.turn()
        x_zero, y_zero = weight_grads(0, dense, dense_b, joined, joined_b)
        both_one = Together(jnp.stack, x_one, y_one)
        both_one.turn()
    else:
        for l in reversed(range(layers)):
            x_all, _, _, _, _, o, _, h, act, _, _ = saved[l]
            dense, dr1, do, vec = dense_part(l, own, far)
            joined, own, far_part = attn_part(l, do, dr1, vec)
            dk, dv, dq = joined[: 2 * rows], joined[2 * rows : 4 * rows], joined[4 * rows :]
            far = flip(far_part)
            du, df, db = dense[:, :ff], dense[:, ff : ff + width], dense[:, ff + width :]
            grads = [
                jnp.concatenate(
                    [over_rows(x_all[:rows], dq), over_rows(x_all, dk), over_rows(x_all, dv),
                     over_rows(o, db)], axis=1,
                ),
                over_rows(h, du),
                over_rows(act, df).reshape(devices, parts, own_rows, width)
                .transpose(0, 2, 1, 3).reshape(width, ff),
            ]
            shards[l] = [
                lax.psum_scatter(g.astype(BF), AXES, scatter_dimension=0, tiled=True).astype(F4)
                for g in grads
            ]
    sums = order(
        lambda one, two: table_sums(key_columns, own_columns, one, two, line_n, plane_n),
        *score_grads,
    )
    heads = sums.shape[0]
    wide = jnp.concatenate([sums[:, n] for n in range(3)], axis=1)
    wide = jnp.pad(wide, ((0, VEC_GRADS - heads), (0, width - wide.shape[1])))
    flat = jnp.concatenate(vec_grads + [wide], axis=0)
    if split:
        both_one.turn()
        small = Everywhere(devices, order, flat)
        x_zero.turn()
        small.step()
        y_zero.turn()
        small.step()
        both_zero = Together(jnp.stack, x_zero, y_zero)
        both_zero.turn(both_one.came)
        far_part, _ = lax.optimization_barrier((far_part, both_zero.keep))
        far = flip(far_part)
        both_zero.turn(far)
        small.step()
        small.step()
        flat = small.total()
        both_zero.came, both_one.came, flat = lax.optimization_barrier(
            (both_zero.came, both_one.came, flat)
        )
        for l, both in ((0, both_zero), (1, both_one)):
            one, two = both.totals()
            shards[l] = [
                jnp.concatenate([one[:, ff:], two[:, ff:]], axis=1), one[:, :ff], two[:, :ff]
            ]
    else:
        flat = summed_everywhere(flat, devices)
    grad_in = (own + far.astype(F4)).astype(BF)
    sums = flat[layers * VEC_GRADS : layers * VEC_GRADS + heads]
    grad_across = buckets_from_sums(sums[:, :LANES], plane_n)
    grad_upward = buckets_from_sums(sums[:, LANES : 2 * LANES], plane_n)
    grad_line = buckets_from_sums(sums[:, 2 * LANES : 3 * LANES], line_n)

    vec_grad = flat[: layers * VEC_GRADS].reshape(layers, VEC_GRADS, width)
    mine = lax.dynamic_slice_in_dim(vec_grad, me * own_rows, own_rows, axis=2)
    grad_in_bias = lax.dynamic_slice_in_dim(
        vec_grad[:, 3 : 3 + parts].reshape(layers, ff), me * parts * own_rows, parts * own_rows, axis=1
    )
    out_bias_g, gain_one_g, shift_one_g = [mine[:, n] for n in range(3)]
    back_bias_g, gain_two_g, shift_two_g = [mine[:, 3 + parts + n] for n in range(3)]
    query_bias_g, value_bias_g = mine[:, VEC_GRADS - 2], mine[:, VEC_GRADS - 1]

    grad_attn = jnp.stack([shards[l][0] for l in range(layers)])
    grad_inw = jnp.stack([shards[l][1] for l in range(layers)])
    grad_back = jnp.stack(
        [
            jnp.concatenate(
                [shards[l][2][:, g * width : (g + 1) * width] for g in range(parts)], axis=0
            )
            for l in range(layers)
        ]
    )
    return (
        hidden_out, grad_in,
        grad_attn[:, :, : 3 * width], query_bias_g, value_bias_g, grad_attn[:, :, 3 * width :],
        out_bias_g, gain_one_g, shift_one_g,
        grad_inw, grad_in_bias, grad_back, back_bias_g, gain_two_g, shift_two_g,
        grad_line, grad_across, grad_upward,
    )


def solution(mesh):
    devices = mesh.shape["dp"] * mesh.shape["blk"]
    tokens = P(AXES, None)
    weight = P(None, AXES, None)
    vector = P(None, AXES)
    return jax.shard_map(
        functools.partial(on_device, devices),
        mesh=mesh,
        in_specs=(
            tokens, tokens, P("dp"), P(None, AXES),
            weight, vector, vector, weight, vector, vector, vector,
            weight, vector, weight, vector, vector, vector,
            P(), P(), P(),
        ),
        out_specs=(
            tokens, tokens,
            weight, vector, vector, weight, vector, vector, vector,
            weight, vector, weight, vector, vector, vector,
            P(), P(), P(),
        ),
        check_vma=False,
    )
```
